32 devices in a mesh: parts: 2 (over x), row: 16 (over z, y, core).
Axes of the slice: x: 2, y: 2, z: 4, core: 2. Of those that a mesh axis runs over, the one named last changes fastest.
Arguments:
- raw_trace: float32 [320, 768, 512], P('row', 'parts'), parts along dimension 1, may hold values from -1200 to 1200
- fir_taps: float32 [32], replicated, may hold values from -1 to 1
- templ_real: bfloat16 [32, 320, 2048], P(None, None, 'row'), may hold values from -6 to 6
- templ_imag: bfloat16 [32, 320, 2048], P(None, None, 'row'), may hold values from -6 to 6
- channel_mask: int32 [320, 2048], P(None, 'row'), may hold values 0 or 1
- moveout: int32 [320, 2048], P(None, 'row'), may hold values from 0 to 63
Outputs:
- peak: float32 [2048, 768], P('row', 'parts'), parts along dimension 1
- best: float32 [768], P('parts'), parts along dimension 0
The draws below stay inside these ranges and needn't reach their ends.
There are 2 independent parts, one for each index of `parts`. The reference program is written for one: setup_inputs(seed, part) draws one part's arguments, and reference() takes and returns one part's arrays. A program takes and returns all parts, laid end to end along the dimension named above; an argument that names none is the same for every part. Nothing has to cross between parts.
All inputs are finite; a program needn't handle non-finite values. No bound on the sum of `channel_mask` on one device may be relied on, other than what follows from the above.
Results may differ from the reference program's by a relative error of at most 0.0015.
Values may be sent and summed in bfloat16 or wider, within the bound.
No kernel may reach another device: no remote copies, remote signals or barrier semaphores. Data moves between devices by JAX's collectives and lax.ppermute only.
A program may use at most 128 MiB of HBM per device.

```python
import math
import jax
import jax.numpy as jnp
from jax import lax

CHANNELS = 320
SAMPLES = 256
BAND_BINS = 32
FIRST_BIN = 16
FILTER_TAPS = 32
MAX_MOVEOUT = 64
WINDOWS = 384
TEMPLATES = 2048


def draw_raw_trace(key, part):
    keys = jax.random.split(key, 3)
    ramp = 3.0 ** (jnp.arange(CHANNELS, dtype=jnp.float32) / max(CHANNELS - 1, 1))
    channel_gain = ramp * jnp.exp(jax.random.uniform(keys[0], (CHANNELS,), jnp.float32, 0.0, math.log(10.0)))
    window_gain = jnp.exp(jax.random.uniform(keys[1], (WINDOWS,), jnp.float32, 0.0, math.log(10.0)))
    shape = (CHANNELS, WINDOWS, 2 * SAMPLES)
    noise = jnp.clip(jax.random.normal(keys[2], shape, jnp.float32), -4.0, 4.0)
    return channel_gain[:, None, None] * window_gain[None, :, None] * noise


def set_ends(entries, rng, low, largest):
    place = [jax.random.randint(jax.random.fold_in(rng, axis), (), 0, length) for axis, length in enumerate(entries.shape)]
    widest = entries.shape.index(max(entries.shape))
    beside = place[:widest] + [(place[widest] + 1) % entries.shape[widest]] + place[widest + 1:]
    return entries.at[tuple(place)].set(low).at[tuple(beside)].set(largest)


def steps_of(key, extent, cuts, smallest, top_value):
    loudness, own = 1.0, jax.random.fold_in(key, 6)
    for axis_at, blocks in cuts:
        heights = jnp.exp(jax.random.uniform(jax.random.fold_in(own, axis_at), (blocks,), jnp.float32, smallest / len(cuts), top_value / len(cuts)))
        loudness = loudness * jnp.repeat(heights, extent[axis_at] // blocks).reshape([-1 if axis == axis_at else 1 for axis in range(len(extent))])
    return loudness


def normal_values(rng, extent, deviation, limit, cuts=(), kind=jnp.bfloat16):
    factor_of = steps_of(rng, extent, cuts, -0.22, 0.18) if cuts else 1.0
    result = jax.random.normal(rng, extent, jnp.float32) * deviation * factor_of
    return jnp.minimum(jnp.maximum(result, -limit), limit).astype(kind)


def setup_inputs(seed: int = 0, part: int = 0) -> dict:
    streams_of = jax.random.split(jax.random.key(seed), 7)
    part_splits = jax.random.split(jax.random.fold_in(streams_of[6], part), 7)
    return {
        "raw_trace": draw_raw_trace(jax.random.fold_in(jax.random.fold_in(streams_of[6], part), 71), part),
        "fir_taps": normal_values(streams_of[1], (FILTER_TAPS,), FILTER_TAPS ** -0.5, 1.0, (), jnp.float32),
        "templ_real": normal_values(streams_of[2], (BAND_BINS, CHANNELS, TEMPLATES), 1.0, 6.0, ((2, 16),)),
        "templ_imag": normal_values(streams_of[3], (BAND_BINS, CHANNELS, TEMPLATES), 1.0, 6.0, ((2, 16),)),
        "channel_mask": set_ends((jax.random.randint(streams_of[4], (CHANNELS, TEMPLATES), 0, 4) < 3).astype(jnp.int32), jax.random.fold_in(streams_of[4], 1), 0, 1),
        "moveout": set_ends(jax.random.randint(streams_of[5], (CHANNELS, TEMPLATES), 0, MAX_MOVEOUT), jax.random.fold_in(streams_of[5], 1), 0, MAX_MOVEOUT - 1).astype(jnp.int32),
    }


epsilon = 1e-06

def reference(raw_trace, fir_taps, templ_real, templ_imag, channel_mask, moveout):
    padded = jnp.pad(raw_trace, ((0, 0), (0, 0), (FILTER_TAPS - 1, 0)))
    decimated = jnp.zeros((CHANNELS, WINDOWS, SAMPLES), jnp.float32)
    for tap in range(FILTER_TAPS):
        begin = FILTER_TAPS - 1 - tap
        decimated = decimated + fir_taps[tap] * padded[:, :, begin:begin + 2 * SAMPLES:2]
    spectrum = jnp.fft.rfft(decimated, axis=-1)[:, :, FIRST_BIN:FIRST_BIN + BAND_BINS]
    spec_real = jnp.transpose(jnp.real(spectrum), (2, 0, 1)).astype(jnp.bfloat16)
    spec_imag = jnp.transpose(jnp.imag(spectrum), (2, 0, 1)).astype(jnp.bfloat16)
    real_wide = spec_real.astype(jnp.float32)
    imag_wide = spec_imag.astype(jnp.float32)
    energy = lax.optimization_barrier(jnp.sum(real_wide * real_wide + imag_wide * imag_wide, axis=(0, 1)))
    data_norm = jnp.sqrt(energy + epsilon)
    bin_index = FIRST_BIN + jnp.arange(BAND_BINS, dtype=jnp.int32)
    lag_index = jnp.arange(SAMPLES, dtype=jnp.int32)
    inverse_angle = 2.0 * math.pi / SAMPLES * (bin_index[:, None] * lag_index[None, :] % SAMPLES).astype(jnp.float32)
    inverse = jnp.concatenate([jnp.cos(inverse_angle), -jnp.sin(inverse_angle)], axis=0)
    scale = math.sqrt(2.0 * CHANNELS * BAND_BINS)
    block = math.gcd(TEMPLATES, 128)
    count = TEMPLATES // block

    def one_block(operands):
        real_block, imag_block, mask_block, shift_block = operands
        shift = bin_index[:, None, None] * shift_block[None, :, :] % SAMPLES
        phase = 2.0 * math.pi / SAMPLES * shift.astype(jnp.float32)
        cosine = jnp.cos(phase)
        sine = jnp.sin(phase)
        weight = mask_block.astype(jnp.float32)[None, :, :]
        real_in = real_block.astype(jnp.float32)
        imag_in = imag_block.astype(jnp.float32)
        eff_real = (weight * (real_in * cosine + imag_in * sine)).astype(jnp.bfloat16).astype(jnp.float32)
        eff_imag = (weight * (imag_in * cosine - real_in * sine)).astype(jnp.bfloat16).astype(jnp.float32)
        templ_norm = jnp.sqrt(lax.optimization_barrier(jnp.sum(eff_real * eff_real + eff_imag * eff_imag, axis=(0, 1))) + epsilon)
        cross_real = jnp.einsum('fct,fcw->ftw', eff_real, real_wide) + jnp.einsum('fct,fcw->ftw', eff_imag, imag_wide)
        cross_imag = jnp.einsum('fct,fcw->ftw', eff_real, imag_wide) - jnp.einsum('fct,fcw->ftw', eff_imag, real_wide)
        joined = jnp.concatenate([cross_real, cross_imag], axis=0)
        stacked = jnp.einsum('ftw,fn->twn', joined, inverse, precision=lax.Precision.HIGHEST)
        highest = lax.optimization_barrier(jnp.max(stacked, axis=2))
        return highest * scale / (templ_norm[:, None] * data_norm[None, :])
    real_blocks = jnp.transpose(templ_real.reshape(BAND_BINS, CHANNELS, count, block), (2, 0, 1, 3))
    imag_blocks = jnp.transpose(templ_imag.reshape(BAND_BINS, CHANNELS, count, block), (2, 0, 1, 3))
    mask_blocks = jnp.transpose(channel_mask.reshape(CHANNELS, count, block), (1, 0, 2))
    shift_blocks = jnp.transpose(moveout.reshape(CHANNELS, count, block), (1, 0, 2))
    peaks = lax.map(one_block, (real_blocks, imag_blocks, mask_blocks, shift_blocks))
    peak = peaks.reshape(TEMPLATES, WINDOWS)
    best = lax.optimization_barrier(jnp.max(peak, axis=0))
    return (peak, best)
```

```python
import math

import jax
import jax.numpy as jnp
import numpy as np
from jax import lax
from jax.experimental import pallas as pl
from jax.experimental.pallas import tpu as pltpu
from jax.sharding import PartitionSpec as P

FIRST_BIN = 16
LANES = 128
HALF = LANES // 2
VMEM_LIMIT = 56 * 2**20

epsilon = 1e-06


def split_three(wide):
    high = wide.astype(jnp.bfloat16)
    rest = wide - high.astype(jnp.float32)
    middle = rest.astype(jnp.bfloat16)
    low = (rest - middle.astype(jnp.float32)).astype(jnp.bfloat16)
    return high, middle, low


def forward_table(samples, band):
    turns = (np.arange(samples)[None, :] * (FIRST_BIN + np.arange(band))[:, None]) % samples
    angles = 2.0 * np.pi / samples * turns
    return np.concatenate([np.cos(angles), -np.sin(angles)], axis=0)


def spectra_kernel(band, core_ref, fir_ref, table_ref, x_ref, pk_ref, ps_ref, qk_ref, qs_ref, w_ref):
    count, windows, raw_length = x_ref.shape
    samples = raw_length // 2
    taps = fir_ref.shape[0]
    rows = 2 * band
    contract_last = (((1,), (1,)), ((), ()))

    @pl.when(pl.program_id(0) == 0)
    def _():
        n = lax.broadcasted_iota(jnp.int32, (samples, raw_length), 0)
        m = lax.broadcasted_iota(jnp.int32, (samples, raw_length), 1)
        offset = 2 * n - m
        filt = jnp.zeros((samples, raw_length), jnp.float32)
        for k in range(taps):
            filt = jnp.where(offset == k, fir_ref[k], filt)
        combined = jnp.dot(
            table_ref[...], filt, precision=lax.Precision.HIGHEST, preferred_element_type=jnp.float32
        )
        for i, piece in enumerate(split_three(combined)):
            w_ref[i * rows : (i + 1) * rows, :] = piece

    first = core_ref[0] == 0
    lane = lax.broadcasted_iota(jnp.int32, (band, LANES), 1)
    wide = windows // 2 // LANES * LANES
    for c in range(count):
        high, middle, low = split_three(x_ref[c])
        one = lax.dot_general(w_ref[...], high, contract_last, preferred_element_type=jnp.float32)
        two = lax.dot_general(w_ref[: 2 * rows], middle, contract_last, preferred_element_type=jnp.float32)
        three = lax.dot_general(w_ref[:rows], low, contract_last, preferred_element_type=jnp.float32)
        small = one[2 * rows :] + two[rows:] + three
        out = one[:rows] + (one[rows : 2 * rows] + two[:rows] + small)
        for j in range(wide // LANES):
            left = out[:, j * LANES : (j + 1) * LANES]
            right = out[:, wide + j * LANES : wide + (j + 1) * LANES]
            pk_ref[c, :, j * LANES : (j + 1) * LANES] = jnp.where(first, left, right).astype(jnp.bfloat16)
            ps_ref[c, :, j * LANES : (j + 1) * LANES] = jnp.where(first, right, left).astype(jnp.bfloat16)
        real = out[:band, 2 * wide :]
        imag = out[band:, 2 * wide :]
        left = jnp.where(lane < HALF, real, pltpu.roll(imag, HALF, 1))
        right = jnp.where(lane < HALF, pltpu.roll(real, HALF, 1), imag)
        qk_ref[c] = jnp.where(first, left, right).astype(jnp.bfloat16)
        qs_ref[c] = jnp.where(first, right, left).astype(jnp.bfloat16)


def spectra_call(raw_trace, fir_taps, core, band):
    channels, windows, raw_length = raw_trace.shape
    samples = raw_length // 2
    step = math.gcd(channels, 4)
    wide = windows // 2 // LANES * LANES
    table = jnp.asarray(forward_table(samples, band), jnp.float32)
    p_shape = (channels, 2 * band, wide)
    q_shape = (channels, band, LANES)
    smem = pl.BlockSpec(memory_space=pltpu.SMEM)

    def block(shape):
        return pl.BlockSpec((step,) + shape[1:], lambda i: (i, 0, 0))

    return pl.pallas_call(
        lambda *refs: spectra_kernel(band, *refs),
        grid=(channels // step,),
        in_specs=[
            smem,
            smem,
            pl.BlockSpec(table.shape, lambda i: (0, 0)),
            block(raw_trace.shape),
        ],
        out_specs=[block(p_shape), block(p_shape), block(q_shape), block(q_shape)],
        out_shape=[jax.ShapeDtypeStruct(s, jnp.bfloat16) for s in (p_shape, p_shape, q_shape, q_shape)],
        scratch_shapes=[pltpu.VMEM((6 * band, raw_length), jnp.bfloat16)],
        compiler_params=pltpu.CompilerParams(vmem_limit_bytes=VMEM_LIMIT),
        name="spectra",
    )(core, fir_taps, table, raw_trace)


def templates_kernel(cos0, sin0, cos1, sin1, real_ref, imag_ref, eff_ref, norm_ref, cos_ref, sin_ref):
    bins, channels, templates = real_ref.shape

    @pl.when(pl.program_id(0) == 0)
    def _():
        cos_ref[...] = cos0[...]
        sin_ref[...] = sin0[...]
        norm_ref[...] = jnp.zeros_like(norm_ref)

    for f in range(bins):
        cosine = cos_ref[...]
        sine = sin_ref[...]
        cos_ref[...] = cosine * cos1[...] - sine * sin1[...]
        sin_ref[...] = sine * cos1[...] + cosine * sin1[...]
        real = real_ref[f].astype(jnp.float32)
        imag = imag_ref[f].astype(jnp.float32)
        eff_real = (real * cosine + imag * sine).astype(jnp.bfloat16).astype(jnp.float32)
        eff_imag = (imag * cosine - real * sine).astype(jnp.bfloat16).astype(jnp.float32)
        norm_ref[...] += jnp.sum(eff_real * eff_real + eff_imag * eff_imag, axis=0, keepdims=True)
        stacked = jnp.concatenate([eff_real, eff_imag], axis=0)
        eff_ref[f] = stacked.T.astype(jnp.bfloat16)


def templates_call(templ_real, templ_imag, channel_mask, moveout, samples):
    band, channels, templates = templ_real.shape
    unit = 2.0 * math.pi / samples
    weight = channel_mask.astype(jnp.float32)
    start = (FIRST_BIN * moveout % samples).astype(jnp.float32) * unit
    turn = (moveout % samples).astype(jnp.float32) * unit
    tables = (weight * jnp.cos(start), weight * jnp.sin(start), jnp.cos(turn), jnp.sin(turn))
    step = math.gcd(band, 4)
    full = pl.BlockSpec((channels, templates), lambda i: (0, 0))
    block = pl.BlockSpec((step, channels, templates), lambda i: (i, 0, 0))
    return pl.pallas_call(
        templates_kernel,
        grid=(band // step,),
        in_specs=[full] * 4 + [block] * 2,
        out_specs=[
            pl.BlockSpec((step, templates, 2 * channels), lambda i: (i, 0, 0)),
            pl.BlockSpec((1, templates), lambda i: (0, 0)),
        ],
        out_shape=[
            jax.ShapeDtypeStruct((band, templates, 2 * channels), jnp.bfloat16),
            jax.ShapeDtypeStruct((1, templates), jnp.float32),
        ],
        scratch_shapes=[pltpu.VMEM((channels, templates), jnp.float32)] * 2,
        compiler_params=pltpu.CompilerParams(vmem_limit_bytes=VMEM_LIMIT),
        name="templates",
    )(*tables, templ_real, templ_imag)


def inverse_table(samples, band):
    table = jnp.asarray(forward_table(samples, band).T, jnp.float32)
    high = table.astype(jnp.bfloat16)
    low = (table - high.astype(jnp.float32)).astype(jnp.bfloat16)
    return jnp.concatenate([high, high, low], axis=1)


def peaks_kernel(
    packed, counts, scale, slot_ref, table_ref, norm_ref, eff_a, eff_b, *refs
):
    arrays = refs[: len(counts)]
    peak_ref, best_ref, staged, spec, cross, eff, sems = refs[len(counts) :]
    channels, rows, lanes = staged.shape
    band = eff.shape[0]
    templates = eff_a.shape[1]
    both = 2 * templates
    part = arrays[0].shape[1] // 2
    eff_copies = [
        pltpu.make_async_copy(eff_a, eff.at[:, pl.ds(0, templates), :], sems.at[0]),
        pltpu.make_async_copy(eff_b, eff.at[:, pl.ds(templates, templates), :], sems.at[1]),
    ]
    for copy in eff_copies:
        copy.start()

    def block_copies(which):
        copies = []
        entry = 0
        for array, count in zip(arrays, counts):
            for j in range(count):
                where = slot_ref[entry]
                for h in range(2):
                    home = slot_ref[len(slot_ref) - 2 + h] if False else (where * 2 + jnp.where(slot_ref[which] == h, 0, 1)) * part
                    copies.append((where >= 0, array, j, h, home))
                entry += 1
        return copies

    total = sum(counts)
    plan = block_copies(total)
    for begin in (True, False):
        for valid, array, j, h, home in plan:

            @pl.when(valid)
            def _():
                copy = pltpu.make_async_copy(
                    array.at[j, pl.ds(h * part, part)], staged.at[pl.ds(home, part)], sems.at[2]
                )
                copy.start() if begin else copy.wait()

    def unpack(c, energy):
        value = staged[c].astype(jnp.float32)
        spec[pl.ds(pl.multiple_of(c * rows, rows), rows), :] = value
        return energy + value * value

    energy = lax.fori_loop(0, channels, unpack, jnp.zeros((rows, lanes), jnp.float32))
    energy = jnp.sum(energy, axis=0, keepdims=True)
    for copy in eff_copies:
        copy.wait()

    lane = lax.broadcasted_iota(jnp.int32, (1, lanes), 1)
    if packed:
        energy = energy + pltpu.roll(energy, HALF, 1)
        group = templates

        def one_bin(f, carry):
            left = spec[pl.ds(f, channels, stride=rows), :]
            right = jnp.where(lane < HALF, 1.0, -1.0) * pltpu.roll(left, HALF, 1)
            values = jnp.concatenate([left, right], axis=0).astype(jnp.bfloat16)
            out = jnp.dot(eff[f], values, preferred_element_type=jnp.float32)
            first, second = out[:group], out[group:]
            real = jnp.where(lane < HALF, first, pltpu.roll(second, HALF, 1))
            imag = jnp.where(lane < HALF, pltpu.roll(first, HALF, 1), second)
            cross[pl.ds(f, group, stride=2 * band), :] = real
            cross[pl.ds(band + f, group, stride=2 * band), :] = imag
            return carry
    else:
        group = both

        def one_bin(f, carry):
            real = spec[pl.ds(f, channels, stride=rows), :].astype(jnp.bfloat16)
            imag = spec[pl.ds(band + f, channels, stride=rows), :].astype(jnp.bfloat16)
            top = jnp.concatenate([real, imag], axis=1)
            bottom = jnp.concatenate([imag, -real], axis=1)
            values = jnp.concatenate([top, bottom], axis=0)
            out = jnp.dot(eff[f], values, preferred_element_type=jnp.float32)
            cross[pl.ds(f, group, stride=2 * band), :] = out[:, :lanes]
            cross[pl.ds(band + f, group, stride=2 * band), :] = out[:, lanes:]
            return carry

    lax.fori_loop(0, band, one_bin, 0)
    depth = 2 * band

    def one_pair(i, carry):
        both_cross = jnp.concatenate(
            [
                cross[pl.ds(pl.multiple_of((2 * i + j) * depth, depth), depth), :] for j in range(2)
            ],
            axis=1,
        )
        high = both_cross.astype(jnp.bfloat16)
        low = (both_cross - high.astype(jnp.float32)).astype(jnp.bfloat16)
        values = jnp.concatenate([high, low, high], axis=0)
        out = jnp.dot(table_ref[...], values, preferred_element_type=jnp.float32)
        top = jnp.max(out, axis=0, keepdims=True)
        peak_ref[pl.ds(2 * i, 1), :] = top[:, :lanes]
        peak_ref[pl.ds(2 * i + 1, 1), :] = top[:, lanes:]
        return carry

    lax.fori_loop(0, group // 2, one_pair, 0, unroll=4)
    data_norm = jnp.sqrt(energy + epsilon)
    norm = norm_ref[...]
    if packed:
        templ_norm = jnp.where(lane < HALF, norm[:group], norm[group:])
    else:
        templ_norm = norm
    peak = peak_ref[...] * scale / (templ_norm * data_norm)
    peak_ref[...] = peak
    best = jnp.max(peak, axis=0, keepdims=True)
    if packed:
        best = jnp.maximum(best, pltpu.roll(best, HALF, 1))
    best_ref[...] = best


def peaks_call(packed, slots, core, arrays, table, templ_norm, eff_a, eff_b, channels):
    counts = tuple(a.shape[0] for a in arrays)
    band, templates, depth = eff_a.shape
    rows, lanes = arrays[0].shape[2:]
    scale = math.sqrt(2.0 * channels * band)
    group = templates if packed else 2 * templates
    smem = pl.BlockSpec(memory_space=pltpu.SMEM)
    vmem = pl.BlockSpec(memory_space=pltpu.VMEM)
    hbm = pl.BlockSpec(memory_space=pl.ANY)
    slot_table = jnp.concatenate([jnp.stack(slots).astype(jnp.int32), core[None].astype(jnp.int32)])
    return pl.pallas_call(
        lambda *refs: peaks_kernel(packed, counts, scale, *refs),
        in_specs=[smem, vmem, vmem, hbm, hbm] + [hbm] * len(arrays),
        out_specs=[vmem, vmem],
        out_shape=[
            jax.ShapeDtypeStruct((group, lanes), jnp.float32),
            jax.ShapeDtypeStruct((1, lanes), jnp.float32),
        ],
        scratch_shapes=[
            pltpu.VMEM((channels, rows, lanes), jnp.bfloat16),
            pltpu.VMEM((channels * rows, lanes), jnp.float32),
            pltpu.VMEM((group * 2 * band, lanes), jnp.float32),
            pltpu.VMEM((band, 2 * templates, depth), jnp.bfloat16),
            pltpu.SemaphoreType.DMA((3,)),
        ],
        compiler_params=pltpu.CompilerParams(vmem_limit_bytes=VMEM_LIMIT),
        name="peaks",
    )(slot_table, table, templ_norm, eff_a, eff_b, *arrays)


class Grid:
    def __init__(self, size):
        self.size = size
        self.core = 2
        outer = size // self.core
        self.y = 2 if outer % 2 == 0 else 1
        self.z = outer // self.y

    def place(self, z, y, c):
        return (z * self.y + y) * self.core + c

    def pairs(self, dz=0, flip_y=False, flip_core=False, keep=lambda z: True):
        found = []
        for z in range(self.z):
            for y in range(self.y):
                for c in range(self.core):
                    if 0 <= z + dz < self.z and keep(z):
                        to = self.place(z + dz, (1 - y) if flip_y else y, (1 - c) if flip_core else c)
                        found.append((self.place(z, y, c), to))
        return found


def body(raw_trace, fir_taps, templ_real, templ_imag, channel_mask, moveout, *, row):
    grid = Grid(row)
    local_channels, windows, raw_length = raw_trace.shape
    samples = raw_length // 2
    band, channels, local_templates = templ_real.shape
    wide = windows // 2 // LANES * LANES
    index = lax.axis_index("row")
    core = index % grid.core
    my_y = index // grid.core % grid.y
    my_z = index // (grid.core * grid.y)

    def send(value, **how):
        return lax.ppermute(value, "row", grid.pairs(**how))

    def swap(value):
        return send(value, flip_core=True)

    p_keep, p_send, q_keep, q_send = spectra_call(
        raw_trace, fir_taps, core[None].astype(jnp.int32), band
    )
    p_own = jnp.concatenate([p_keep, swap(p_send)], axis=0)[None]
    q_own = jnp.concatenate([q_keep, swap(q_send)], axis=0)[None]

    eff, norm = templates_call(templ_real, templ_imag, channel_mask, moveout, samples)
    eff_other = swap(eff)
    norm_pair = jnp.stack([norm[0], swap(norm)[0]])

    def gather(own):
        arrays = [own]
        slots = [my_z * grid.y + my_y]
        if grid.y == 2:
            arrays.append(send(own, flip_y=True))
            slots.append(my_z * grid.y + 1 - my_y)
        up = down = own
        for s in range(1, grid.z):
            up = send(up, dz=1, keep=lambda z: z >= s - 1)
            down = send(down, dz=-1, keep=lambda z: z <= grid.z - s)
            for value, from_z, has in (
                (up, my_z - s, lambda z: z >= s),
                (down, my_z + s, lambda z: z <= grid.z - 1 - s),
            ):
                valid = (from_z >= 0) & (from_z < grid.z)
                arrays.append(value)
                slots.append(jnp.where(valid, from_z * grid.y + my_y, -1))
                if grid.y == 2:
                    arrays.append(send(value, flip_y=True, keep=has))
                    slots.append(jnp.where(valid, from_z * grid.y + 1 - my_y, -1))
        return arrays, slots

    table = inverse_table(samples, band)
    templ_norm = jnp.sqrt(norm_pair + epsilon).reshape(2 * local_templates, 1)
    p_arrays, slots = gather(p_own)
    q_arrays, _ = gather(q_own)
    p_peak, p_best = peaks_call(False, slots, core, p_arrays, table, templ_norm, eff, eff_other, channels)
    q_peak, q_best = peaks_call(True, slots, core, q_arrays, table, templ_norm, eff, eff_other, channels)

    p_other = swap(p_peak[local_templates:])
    q_other = swap(q_peak[:, HALF:])
    q_mine = q_peak[:, :HALF]
    p_mine = p_peak[:local_templates]
    first = core == 0
    peak = jnp.concatenate(
        [
            jnp.where(first, p_mine, p_other),
            jnp.where(first, p_other, p_mine),
            jnp.where(first, q_mine, q_other),
            jnp.where(first, q_other, q_mine),
        ],
        axis=1,
    )

    mine = jnp.concatenate([p_best, q_best], axis=1)
    distance = 1
    if grid.y == 2:
        mine = jnp.maximum(mine, send(mine, flip_y=True))
    if grid.z & (grid.z - 1) == 0:
        while distance < grid.z:
            pairs = [
                (grid.place(z, y, c), grid.place(z ^ distance, y, c))
                for z in range(grid.z)
                for y in range(grid.y)
                for c in range(grid.core)
            ]
            mine = jnp.maximum(mine, lax.ppermute(mine, "row", pairs))
            distance *= 2
    else:
        mine = lax.pmax(mine, "row")
    other = swap(mine)
    one = jnp.where(first, mine, other)[0]
    two = jnp.where(first, other, mine)[0]
    best = jnp.concatenate(
        [one[:wide], two[:wide], one[wide : wide + HALF], two[wide : wide + HALF]]
    )
    return (peak, best)


def solution(mesh):
    in_specs = (
        P("row", "parts", None),
        P(),
        P(None, None, "row"),
        P(None, None, "row"),
        P(None, "row"),
        P(None, "row"),
    )
    out_specs = (P("row", "parts"), P("parts"))
    row = mesh.shape["row"]

    def local(*args):
        return body(*args, row=row)

    return jax.shard_map(local, mesh=mesh, in_specs=in_specs, out_specs=out_specs, check_vma=False)
```

```python
import math

import jax
import jax.numpy as jnp
import numpy as np
from jax import lax
from jax.experimental import pallas as pl
from jax.experimental.pallas import tpu as pltpu
from jax.sharding import PartitionSpec as P

FIRST_BIN = 16
LANES = 128
HALF = LANES // 2
SKEW = 8
VMEM_LIMIT = 56 * 2**20

epsilon = 1e-06


def cost(microseconds):
    return pl.CostEstimate(flops=0, bytes_accessed=int(microseconds * 3e6), transcendentals=0)


def split_three(wide):
    high = wide.astype(jnp.bfloat16)
    rest = wide - high.astype(jnp.float32)
    middle = rest.astype(jnp.bfloat16)
    low = (rest - middle.astype(jnp.float32)).astype(jnp.bfloat16)
    return high, middle, low


def forward_table(samples, band):
    turns = (np.arange(samples)[None, :] * (FIRST_BIN + np.arange(band))[:, None]) % samples
    angles = 2.0 * np.pi / samples * turns
    return np.concatenate([np.cos(angles), -np.sin(angles)], axis=0)


def spectra_kernel(band, core_ref, fir_ref, table_ref, x_ref, pk_ref, ps_ref, qk_ref, qs_ref, w_ref):
    count, windows, raw_length = x_ref.shape
    samples = raw_length // 2
    taps = fir_ref.shape[0]
    rows = 2 * band
    contract_last = (((1,), (1,)), ((), ()))

    @pl.when(pl.program_id(0) == 0)
    def _():
        n = lax.broadcasted_iota(jnp.int32, (samples, raw_length), 0)
        m = lax.broadcasted_iota(jnp.int32, (samples, raw_length), 1)
        offset = 2 * n - m
        filt = jnp.zeros((samples, raw_length), jnp.float32)
        for k in range(taps):
            filt = jnp.where(offset == k, fir_ref[k], filt)
        combined = jnp.dot(
            table_ref[...], filt, precision=lax.Precision.HIGHEST, preferred_element_type=jnp.float32
        )
        for i, piece in enumerate(split_three(combined)):
            w_ref[i * rows : (i + 1) * rows, :] = piece

    first = core_ref[0] == 0
    lane = lax.broadcasted_iota(jnp.int32, (band, LANES), 1)
    wide = windows // 2 // LANES * LANES
    for c in range(count):
        high, middle, low = split_three(x_ref[c])
        one = lax.dot_general(w_ref[...], high, contract_last, preferred_element_type=jnp.float32)
        two = lax.dot_general(w_ref[: 2 * rows], middle, contract_last, preferred_element_type=jnp.float32)
        three = lax.dot_general(w_ref[:rows], low, contract_last, preferred_element_type=jnp.float32)
        small = one[2 * rows :] + two[rows:] + three
        out = one[:rows] + (one[rows : 2 * rows] + two[:rows] + small)
        for j in range(wide // LANES):
            left = out[:, j * LANES : (j + 1) * LANES]
            right = out[:, wide + j * LANES : wide + (j + 1) * LANES]
            pk_ref[c, :, j * LANES : (j + 1) * LANES] = jnp.where(first, left, right).astype(jnp.bfloat16)
            ps_ref[c, :, j * LANES : (j + 1) * LANES] = jnp.where(first, right, left).astype(jnp.bfloat16)
        real = out[:band, 2 * wide :]
        imag = out[band:, 2 * wide :]
        left = jnp.where(lane < HALF, real, pltpu.roll(imag, HALF, 1))
        right = jnp.where(lane < HALF, pltpu.roll(real, HALF, 1), imag)
        qk_ref[c] = jnp.where(first, left, right).astype(jnp.bfloat16)
        qs_ref[c] = jnp.where(first, right, left).astype(jnp.bfloat16)


def spectra_call(raw_trace, fir_taps, core, band):
    channels, windows, raw_length = raw_trace.shape
    samples = raw_length // 2
    step = math.gcd(channels, 4)
    wide = windows // 2 // LANES * LANES
    table = jnp.asarray(forward_table(samples, band), jnp.float32)
    p_shape = (channels, 2 * band, wide)
    q_shape = (channels, band, LANES)
    smem = pl.BlockSpec(memory_space=pltpu.SMEM)

    def block(shape):
        return pl.BlockSpec((step,) + shape[1:], lambda i: (i, 0, 0))

    return pl.pallas_call(
        lambda *refs: spectra_kernel(band, *refs),
        grid=(channels // step,),
        in_specs=[
            smem,
            smem,
            pl.BlockSpec(table.shape, lambda i: (0, 0)),
            block(raw_trace.shape),
        ],
        out_specs=[block(p_shape), block(p_shape), block(q_shape), block(q_shape)],
        out_shape=[jax.ShapeDtypeStruct(s, jnp.bfloat16) for s in (p_shape, p_shape, q_shape, q_shape)],
        scratch_shapes=[pltpu.VMEM((6 * band, raw_length), jnp.bfloat16)],
        compiler_params=pltpu.CompilerParams(vmem_limit_bytes=VMEM_LIMIT),
        cost_estimate=cost(10),
        name="spectra",
    )(core, fir_taps, table, raw_trace)


def round_up(value, unit):
    return -(-value // unit) * unit


def templates_kernel(
    early, order_ref, cos0, sin0, cos1, sin1, real_ref, imag_ref,
    eff1_ref, eff2_ref, norm_ref, cos_ref, sin_ref, stage1, stage2,
):
    bins, channels, templates = real_ref.shape
    chips = order_ref.shape[0]
    per_chip = channels // chips

    @pl.when(pl.program_id(0) == 0)
    def _():
        cos_ref[...] = cos0[...]
        sin_ref[...] = sin0[...]
        norm_ref[...] = jnp.zeros_like(norm_ref)
        stage1[...] = jnp.zeros_like(stage1)
        stage2[...] = jnp.zeros_like(stage2)

    for f in range(bins):
        total = jnp.zeros((1, templates), jnp.float32)
        real_all = real_ref[f].astype(jnp.float32)
        imag_all = imag_ref[f].astype(jnp.float32)
        cosine = cos_ref[...]
        sine = sin_ref[...]
        cos_ref[...] = cosine * cos1[...] - sine * sin1[...]
        sin_ref[...] = sine * cos1[...] + cosine * sin1[...]
        eff_real = (real_all * cosine + imag_all * sine).astype(jnp.bfloat16).astype(jnp.float32)
        eff_imag = (imag_all * cosine - real_all * sine).astype(jnp.bfloat16).astype(jnp.float32)
        total += jnp.sum(eff_real * eff_real + eff_imag * eff_imag, axis=0, keepdims=True)
        norm_ref[...] += total
        for j in range(chips):
            at = order_ref[j]
            rows_real = eff_real[j * per_chip : (j + 1) * per_chip]
            rows_imag = eff_imag[j * per_chip : (j + 1) * per_chip]

            @pl.when(at < early)
            def _():
                half = stage1.shape[0] // 2
                stage1[pl.ds(at * per_chip, per_chip), :] = rows_real
                stage1[pl.ds(half + at * per_chip, per_chip), :] = rows_imag

            @pl.when(at >= early)
            def _():
                half = stage2.shape[0] // 2
                stage2[pl.ds((at - early) * per_chip, per_chip), :] = rows_real
                stage2[pl.ds(half + (at - early) * per_chip, per_chip), :] = rows_imag

        eff1_ref[f] = stage1[...].T.astype(jnp.bfloat16)
        eff2_ref[f] = stage2[...].T.astype(jnp.bfloat16)


def templates_call(templ_real, templ_imag, channel_mask, moveout, samples, order, early):
    band, channels, templates = templ_real.shape
    chips = order.shape[0]
    depths = [
        2 * round_up(n * (channels // chips), LANES) for n in (early, chips - early)
    ]
    unit = 2.0 * math.pi / samples
    weight = channel_mask.astype(jnp.float32)
    start = (FIRST_BIN * moveout % samples).astype(jnp.float32) * unit
    turn = (moveout % samples).astype(jnp.float32) * unit
    tables = (weight * jnp.cos(start), weight * jnp.sin(start), jnp.cos(turn), jnp.sin(turn))
    step = math.gcd(band, 4)
    full = pl.BlockSpec((channels, templates), lambda i: (0, 0))
    block = pl.BlockSpec((step, channels, templates), lambda i: (i, 0, 0))
    return pl.pallas_call(
        lambda *refs: templates_kernel(early, *refs),
        grid=(band // step,),
        in_specs=[pl.BlockSpec(memory_space=pltpu.SMEM)] + [full] * 4 + [block] * 2,
        out_specs=[pl.BlockSpec((step, templates, d), lambda i: (i, 0, 0)) for d in depths]
        + [pl.BlockSpec((1, templates), lambda i: (0, 0))],
        out_shape=[jax.ShapeDtypeStruct((band, templates, d), jnp.bfloat16) for d in depths]
        + [jax.ShapeDtypeStruct((1, templates), jnp.float32)],
        scratch_shapes=[pltpu.VMEM((channels, templates), jnp.float32)] * 2
        + [pltpu.VMEM((d, templates), jnp.float32) for d in depths],
        compiler_params=pltpu.CompilerParams(vmem_limit_bytes=VMEM_LIMIT),
        cost_estimate=cost(12),
        name="templates",
    )(order, *tables, templ_real, templ_imag)


def inverse_table(samples, band):
    table = jnp.asarray(forward_table(samples, band).T, jnp.float32)
    high = table.astype(jnp.bfloat16)
    low = (table - high.astype(jnp.float32)).astype(jnp.bfloat16)
    return jnp.concatenate([high, high, low], axis=1)


def unpack_blocks(blocks, spec, pitch):
    rows, lanes = blocks[0].shape[1:]
    padded = spec.shape[0] // pitch
    energy = jnp.zeros((rows, lanes), jnp.float32)
    first = 0
    for block in blocks:
        count = block.shape[0]

        def unpack(c, energy, block=block, first=first):
            value = block[c].astype(jnp.float32)
            spec[pl.ds(pl.multiple_of((first + c) * pitch, 8), rows), :] = value
            return energy + value * value

        energy = lax.fori_loop(0, count, unpack, energy, unroll=math.gcd(count, 10))
        first += count

    def clear(c, carry):
        spec[pl.ds(pl.multiple_of(c * pitch, 8), rows), :] = jnp.zeros((rows, lanes), jnp.float32)
        return carry

    lax.fori_loop(first, padded, clear, 0)
    return jnp.sum(energy, axis=0, keepdims=True)


def cross_of(packed, eff_a, eff_b, spec, pitch, f, bin_at, band):
    padded = spec.shape[0] // pitch
    lane = lax.broadcasted_iota(jnp.int32, (1, LANES), 1)
    if packed:
        left = spec[pl.ds(bin_at, padded, stride=pitch), :]
        right = jnp.where(lane < HALF, 1.0, -1.0) * pltpu.roll(left, HALF, 1)
        values = jnp.concatenate([left, right], axis=0).astype(jnp.bfloat16)
    else:
        real = spec[pl.ds(bin_at, padded, stride=pitch), :].astype(jnp.bfloat16)
        imag = spec[pl.ds(band + bin_at, padded, stride=pitch), :].astype(jnp.bfloat16)
        top = jnp.concatenate([real, imag], axis=1)
        bottom = jnp.concatenate([imag, -real], axis=1)
        values = jnp.concatenate([top, bottom], axis=0)
    eff = jnp.concatenate([eff_a[f], eff_b[f]], axis=0)
    return jnp.dot(eff, values, preferred_element_type=jnp.float32)


def early_kernel(packed, band, count, *refs):
    blocks = refs[:count]
    eff_a, eff_b, cross_ref, energy_ref, spec = refs[count:]
    rows = blocks[0].shape[1]
    pitch = rows + SKEW
    step = pl.program_id(0)

    @pl.when(step == 0)
    def _():
        energy_ref[...] = unpack_blocks(blocks, spec, pitch)

    bins = eff_a.shape[0]
    for f in range(bins):
        cross_ref[f] = cross_of(packed, eff_a, eff_b, spec, pitch, f, step * bins + f, band)


def late_kernel(packed, band, count, scale, *refs):
    blocks = refs[:count]
    (
        eff_a, eff_b, partial_ref, energy_in, norm_ref, table_ref, peak_ref, best_ref, spec, cross, energy_ref,
    ) = refs[count:]
    rows = blocks[0].shape[1]
    pitch = rows + SKEW
    lanes = LANES
    step = pl.program_id(0)
    bins, templates, _ = eff_a.shape
    group = templates if packed else 2 * templates
    depth = 2 * band
    lane = lax.broadcasted_iota(jnp.int32, (1, lanes), 1)

    @pl.when(step == 0)
    def _():
        energy_ref[...] = energy_in[...] + unpack_blocks(blocks, spec, pitch)

    for f in range(bins):
        at = step * bins + f
        out = partial_ref[f] + cross_of(packed, eff_a, eff_b, spec, pitch, f, at, band)
        if packed:
            first, second = out[:group], out[group:]
            real = jnp.where(lane < HALF, first, pltpu.roll(second, HALF, 1))
            imag = jnp.where(lane < HALF, pltpu.roll(first, HALF, 1), second)
        else:
            real, imag = out[:, :lanes], out[:, lanes:]
        cross[pl.ds(at, group, stride=depth), :] = real
        cross[pl.ds(band + at, group, stride=depth), :] = imag

    @pl.when(step == pl.num_programs(0) - 1)
    def _():
        def one_pair(i, carry):
            pair = jnp.concatenate(
                [
                    cross[pl.ds(pl.multiple_of((2 * i + j) * depth, depth), depth), :]
                    for j in range(2)
                ],
                axis=1,
            )
            high = pair.astype(jnp.bfloat16)
            low = (pair - high.astype(jnp.float32)).astype(jnp.bfloat16)
            values = jnp.concatenate([high, low, high], axis=0)
            out = jnp.dot(table_ref[...], values, preferred_element_type=jnp.float32)
            top = jnp.max(out, axis=0, keepdims=True)
            peak_ref[pl.ds(2 * i, 1), :] = top[:, :lanes]
            peak_ref[pl.ds(2 * i + 1, 1), :] = top[:, lanes:]
            return carry

        lax.fori_loop(0, group // 2, one_pair, 0, unroll=math.gcd(group // 2, 16))
        energy = energy_ref[...]
        norm = norm_ref[...]
        if packed:
            energy = energy + pltpu.roll(energy, HALF, 1)
            templ_norm = jnp.where(lane < HALF, norm[:group], norm[group:])
        else:
            templ_norm = norm
        data_norm = jnp.sqrt(energy + epsilon)
        peak = peak_ref[...] * scale / (templ_norm * data_norm)
        peak_ref[...] = peak
        best = jnp.max(peak, axis=0, keepdims=True)
        if packed:
            best = jnp.maximum(best, pltpu.roll(best, HALF, 1))
        best_ref[...] = best


def whole_block(array):
    return pl.BlockSpec(array.shape, lambda i: (0,) * array.ndim, pipeline_mode=pl.Buffered(1))


def early_call(packed, blocks, eff_a, eff_b):
    band, templates, depth = eff_a.shape
    rows = blocks[0].shape[1]
    step = math.gcd(band, 4)
    wide = LANES if packed else 2 * LANES
    eff_spec = pl.BlockSpec((step, templates, depth), lambda i: (i, 0, 0))
    return pl.pallas_call(
        lambda *refs: early_kernel(packed, band, len(blocks), *refs),
        grid=(band // step,),
        in_specs=[whole_block(b) for b in blocks] + [eff_spec] * 2,
        out_specs=[
            pl.BlockSpec((step, 2 * templates, wide), lambda i: (i, 0, 0)),
            pl.BlockSpec((1, LANES), lambda i: (0, 0)),
        ],
        out_shape=[
            jax.ShapeDtypeStruct((band, 2 * templates, wide), jnp.float32),
            jax.ShapeDtypeStruct((1, LANES), jnp.float32),
        ],
        scratch_shapes=[pltpu.VMEM((depth // 2 * (rows + SKEW), LANES), jnp.float32)],
        compiler_params=pltpu.CompilerParams(vmem_limit_bytes=VMEM_LIMIT),
        cost_estimate=cost(10),
        name="early",
    )(*blocks, eff_a, eff_b)


def late_call(packed, blocks, eff_a, eff_b, partial, energy, norm, table, scale):
    band, templates, depth = eff_a.shape
    rows = blocks[0].shape[1]
    step = math.gcd(band, 4)
    group = templates if packed else 2 * templates
    eff_spec = pl.BlockSpec((step, templates, depth), lambda i: (i, 0, 0))
    return pl.pallas_call(
        lambda *refs: late_kernel(packed, band, len(blocks), scale, *refs),
        grid=(band // step,),
        in_specs=[whole_block(b) for b in blocks]
        + [eff_spec] * 2
        + [pl.BlockSpec((step,) + partial.shape[1:], lambda i: (i, 0, 0))]
        + [whole_block(a) for a in (energy, norm, table)],
        out_specs=[
            pl.BlockSpec((group, LANES), lambda i: (0, 0)),
            pl.BlockSpec((1, LANES), lambda i: (0, 0)),
        ],
        out_shape=[
            jax.ShapeDtypeStruct((group, LANES), jnp.float32),
            jax.ShapeDtypeStruct((1, LANES), jnp.float32),
        ],
        scratch_shapes=[
            pltpu.VMEM((depth // 2 * (rows + SKEW), LANES), jnp.float32),
            pltpu.VMEM((group * 2 * band, LANES), jnp.float32),
            pltpu.VMEM((1, LANES), jnp.float32),
        ],
        compiler_params=pltpu.CompilerParams(vmem_limit_bytes=VMEM_LIMIT),
        cost_estimate=cost(14),
        name="late",
    )(*blocks, eff_a, eff_b, partial, energy, norm, table)


class Grid:
    def __init__(self, size):
        self.size = size
        self.core = 2
        outer = size // self.core
        self.y = 2 if outer % 2 == 0 else 1
        self.z = outer // self.y

    def place(self, z, y, c):
        return (z * self.y + y) * self.core + c

    @property
    def chips(self):
        return self.z * self.y

    def ring(self):
        turn = [z * self.y for z in range(self.z)]
        if self.y == 2:
            turn += [z * 2 + 1 for z in reversed(range(self.z))]
        return turn

    def ring_pairs(self, sign):
        turn = self.ring()
        return [
            (turn[i] * self.core + c, turn[(i + sign) % len(turn)] * self.core + c)
            for i in range(len(turn))
            for c in range(self.core)
        ]

    def swap_pairs(self):
        return [(i, i ^ 1) for i in range(self.size)]

    def z_pairs(self, distance):
        return [
            (self.place(z, y, c), self.place(z ^ distance, y, c))
            for z in range(self.z)
            for y in range(self.y)
            for c in range(self.core)
        ]

    def y_pairs(self):
        return [
            (self.place(z, y, c), self.place(z, 1 - y, c))
            for z in range(self.z)
            for y in range(self.y)
            for c in range(self.core)
        ]


def body(raw_trace, fir_taps, templ_real, templ_imag, channel_mask, moveout, *, row):
    grid = Grid(row)
    chips = grid.chips
    local_channels, windows, raw_length = raw_trace.shape
    samples = raw_length // 2
    band, channels, local_templates = templ_real.shape
    wide = windows // 2 // LANES * LANES
    index = lax.axis_index("row")
    core = index % grid.core
    first = core == 0

    def swap(value):
        return lax.ppermute(value, "row", grid.swap_pairs())

    p_keep, p_send, q_keep, q_send = spectra_call(
        raw_trace, fir_taps, core[None].astype(jnp.int32), band
    )
    p_got, q_got = swap(p_send), swap(q_send)

    def chip_block(keep, got):
        return jnp.stack([jnp.where(first, keep, got), jnp.where(first, got, keep)])

    p_own = chip_block(p_keep, p_got)
    q_own = chip_block(q_keep, q_got)

    turn = np.asarray(grid.ring())
    arrival = [0]
    for s in range(1, (chips - 1) // 2 + 1):
        arrival += [-s, s]
    if chips % 2 == 0:
        arrival.append(chips // 2)
    last_step = chips // 2
    early_steps = chips // 4
    early = 1 + 2 * early_steps
    rank = np.zeros((chips, chips), np.int32)
    for i in range(chips):
        for k, away in enumerate(arrival):
            rank[turn[i], turn[(i + away) % chips]] = k
    order = jnp.asarray(rank)[index // grid.core]

    templ_real, templ_imag, channel_mask, moveout, p_own = lax.optimization_barrier(
        (templ_real, templ_imag, channel_mask, moveout, p_own)
    )
    eff1, eff2, norm = templates_call(
        templ_real, templ_imag, channel_mask, moveout, samples, order, early
    )
    table = inverse_table(samples, band)
    scale = math.sqrt(2.0 * channels * band)

    def forth(value):
        return lax.ppermute(value, "row", grid.ring_pairs(1))

    def back(value):
        return lax.ppermute(value, "row", grid.ring_pairs(-1))

    def flat(block):
        return block.reshape((-1,) + block.shape[-2:])

    def step(up, down, s):
        if 2 * s == chips:
            return forth(up[0]), back(down[1])
        return forth(up), back(down)

    def early_part(packed, blocks):
        return early_call(packed, [flat(b) for b in blocks], eff1, eff1_other)

    def late_part(packed, blocks, partial, energy):
        return late_call(
            packed, [flat(b) for b in blocks], eff2, eff2_other, partial, energy, templ_norm, table, scale
        )

    p_blocks, q_blocks = [p_own], [q_own]
    p_up = p_down = p_own
    q_up = q_down = q_own
    for s in range(1, last_step + 1):
        p_up, p_down = step(p_up, p_down, s)
        p_blocks += [p_up, p_down]
        if s == 1:
            q_up, q_down, p_up, p_down, eff1, eff2, norm = lax.optimization_barrier(
                (q_up, q_down, p_up, p_down, eff1, eff2, norm)
            )
            eff1_other, eff2_other = swap(eff1), swap(eff2)
            norm_pair = jnp.stack([norm[0], swap(norm)[0]])
            templ_norm = jnp.sqrt(norm_pair + epsilon).reshape(2 * local_templates, 1)
        if s == last_step - 1:
            p_early = early_part(False, p_blocks[:early])
            p_up, p_down, p_early = lax.optimization_barrier((p_up, p_down, p_early))
    p_peak, p_best = late_part(False, p_blocks[early:], *p_early)
    for s in range(1, last_step + 1):
        q_up, q_down = step(q_up, q_down, s)
        q_blocks += [q_up, q_down]
        if s == 1:
            q_up, q_down, p_early = lax.optimization_barrier((q_up, q_down, p_early))
        if s == last_step - 1:
            q_up, q_down, p_peak = lax.optimization_barrier((q_up, q_down, p_peak))
    q_early = early_part(True, q_blocks[:early])
    q_peak, q_best = late_part(True, q_blocks[early:], *q_early)

    p_other = swap(p_peak[local_templates:])
    q_other = swap(q_peak[:, HALF:])
    q_mine = q_peak[:, :HALF]
    p_mine = p_peak[:local_templates]
    peak = jnp.concatenate(
        [
            jnp.where(first, p_mine, p_other),
            jnp.where(first, p_other, p_mine),
            jnp.where(first, q_mine, q_other),
            jnp.where(first, q_other, q_mine),
        ],
        axis=1,
    )

    mine = jnp.concatenate([p_best, q_best], axis=1)
    if grid.y == 2:
        mine = jnp.maximum(mine, lax.ppermute(mine, "row", grid.y_pairs()))
    if grid.z & (grid.z - 1) == 0:
        distance = 1
        while distance < grid.z:
            mine = jnp.maximum(mine, lax.ppermute(mine, "row", grid.z_pairs(distance)))
            distance *= 2
    else:
        mine = lax.pmax(mine, "row")
    other = swap(mine)
    one = jnp.where(first, mine, other)[0]
    two = jnp.where(first, other, mine)[0]
    best = jnp.concatenate(
        [one[:wide], two[:wide], one[wide : wide + HALF], two[wide : wide + HALF]]
    )
    return (peak, best)


def solution(mesh):
    in_specs = (
        P("row", "parts", None),
        P(),
        P(None, None, "row"),
        P(None, None, "row"),
        P(None, "row"),
        P(None, "row"),
    )
    out_specs = (P("row", "parts"), P("parts"))
    row = mesh.shape["row"]

    def local(*args):
        return body(*args, row=row)

    return jax.shard_map(local, mesh=mesh, in_specs=in_specs, out_specs=out_specs, check_vma=False)
```

```python
import math

import jax
import jax.numpy as jnp
import numpy as np
from jax import lax
from jax.experimental import pallas as pl
from jax.experimental.pallas import tpu as pltpu
from jax.sharding import PartitionSpec as P

FIRST_BIN = 16
LANES = 128
HALF = LANES // 2
SKEW = 8
WIDE_LIMIT = 31 * 2**20
PACKED_LIMIT = 19 * 2**20
LATE_LIMIT = 40 * 2**20
STREAM_LIMIT = 56 * 2**20

epsilon = 1e-06


def cost(microseconds):
    return pl.CostEstimate(flops=0, bytes_accessed=int(microseconds * 3e6), transcendentals=0)


def split_three(wide):
    high = wide.astype(jnp.bfloat16)
    rest = wide - high.astype(jnp.float32)
    middle = rest.astype(jnp.bfloat16)
    low = (rest - middle.astype(jnp.float32)).astype(jnp.bfloat16)
    return high, middle, low


def forward_table(samples, band):
    turns = (np.arange(samples)[None, :] * (FIRST_BIN + np.arange(band))[:, None]) % samples
    angles = 2.0 * np.pi / samples * turns
    return np.concatenate([np.cos(angles), -np.sin(angles)], axis=0)


def spectra_kernel(packed, band, core_ref, fir_ref, table_ref, x_ref, keep_ref, send_ref, w_ref):
    count, windows, raw_length = x_ref.shape
    samples = raw_length // 2
    taps = fir_ref.shape[0]
    rows = 2 * band

    @pl.when(pl.program_id(0) == 0)
    def _():
        lane = lax.broadcasted_iota(jnp.int32, (8, raw_length), 1)
        base = jnp.zeros((8, raw_length), jnp.float32)
        for k in range(taps):
            base = jnp.where(lane == (raw_length - k) % raw_length, fir_ref[k], base)
        turned = pltpu.roll(
            jnp.concatenate([base] * (samples // 8), axis=0), 0, 1, stride=2, stride_axis=0
        )
        n = lax.broadcasted_iota(jnp.int32, (samples, raw_length), 0)
        m = lax.broadcasted_iota(jnp.int32, (samples, raw_length), 1)
        filt = jnp.where(m <= 2 * n, turned, 0.0)
        combined = jnp.dot(
            table_ref[...], filt, precision=lax.Precision.HIGHEST, preferred_element_type=jnp.float32
        )
        high, middle, low = (piece.astype(jnp.float32) for piece in split_three(combined))
        none = jnp.zeros_like(high)
        for i, pair in enumerate(((high, middle), (low, none), (high, none))):
            turned_pair = jnp.concatenate(pair, axis=0).T.astype(jnp.bfloat16)
            w_ref[:, 2 * i * rows : 2 * (i + 1) * rows] = turned_pair

    first = core_ref[0] == 0
    lane = lax.broadcasted_iota(jnp.int32, (band, LANES), 1)
    for c in range(count):
        high, middle, low = split_three(x_ref[c])
        one = jnp.dot(high, w_ref[:, : 4 * rows], preferred_element_type=jnp.float32)
        two = jnp.dot(middle, w_ref[:, : 2 * rows], preferred_element_type=jnp.float32)
        three = jnp.dot(low, w_ref[:, 4 * rows :], preferred_element_type=jnp.float32)
        total = (((one[:, 2 * rows :] + three) + two) + one[:, : 2 * rows]).T
        out = total[:rows] + total[rows:]
        if packed:
            real, imag = out[:band], out[band:]
            left = jnp.where(lane < HALF, real, pltpu.roll(imag, HALF, 1))
            right = jnp.where(lane < HALF, pltpu.roll(real, HALF, 1), imag)
        else:
            left, right = out[:, : windows // 2], out[:, windows // 2 :]
        keep_ref[c] = jnp.where(first, left, right).astype(jnp.bfloat16)
        send_ref[c] = jnp.where(first, right, left).astype(jnp.bfloat16)


def spectra_call(packed, raw_trace, fir_taps, core, band):
    channels, windows, raw_length = raw_trace.shape
    samples = raw_length // 2
    step = math.gcd(channels, 5)
    wide = windows - LANES
    table = jnp.asarray(forward_table(samples, band), jnp.float32)
    shape = (channels, band, LANES) if packed else (channels, 2 * band, wide // 2)
    taken = (step, LANES if packed else wide, raw_length)
    at = wide // LANES if packed else 0
    smem = pl.BlockSpec(memory_space=pltpu.SMEM)
    out_block = pl.BlockSpec((step,) + shape[1:], lambda i: (i, 0, 0))
    return pl.pallas_call(
        lambda *refs: spectra_kernel(packed, band, *refs),
        grid=(channels // step,),
        in_specs=[
            smem,
            smem,
            pl.BlockSpec(table.shape, lambda i: (0, 0)),
            pl.BlockSpec(taken, lambda i: (i, at, 0)),
        ],
        out_specs=[out_block] * 2,
        out_shape=[jax.ShapeDtypeStruct(shape, jnp.bfloat16)] * 2,
        scratch_shapes=[pltpu.VMEM((raw_length, 12 * band), jnp.bfloat16)],
        compiler_params=pltpu.CompilerParams(vmem_limit_bytes=STREAM_LIMIT),
        cost_estimate=cost(5 if packed else 8),
        name="spectra",
    )(core, fir_taps, table, raw_trace)


def round_up(value, unit):
    return -(-value // unit) * unit


def templates_kernel(
    real_at, imag_at, cos0, sin0, cos1, sin1, real_ref, imag_ref,
    eff1_ref, eff2_ref, norm_ref, cos_ref, sin_ref, stage,
):
    bins, channels, templates = real_ref.shape
    chips = real_at.shape[0]
    per_chip = channels // chips
    unit = math.gcd(per_chip, 8)
    split = eff1_ref.shape[2]

    @pl.when(pl.program_id(0) == 0)
    def _():
        cos_ref[...] = cos0[...]
        sin_ref[...] = sin0[...]
        norm_ref[...] = jnp.zeros_like(norm_ref)
        stage[...] = jnp.zeros_like(stage)

    for f in range(bins):
        power = jnp.zeros((per_chip, templates), jnp.float32)
        for j in range(chips):
            here = pl.ds(j * per_chip, per_chip)
            cosine, sine = cos_ref[here, :], sin_ref[here, :]
            cos_ref[here, :] = cosine * cos1[here, :] - sine * sin1[here, :]
            sin_ref[here, :] = sine * cos1[here, :] + cosine * sin1[here, :]
            real = real_ref[f, here, :].astype(jnp.float32)
            imag = imag_ref[f, here, :].astype(jnp.float32)
            eff_real = (real * cosine + imag * sine).astype(jnp.bfloat16).astype(jnp.float32)
            eff_imag = (imag * cosine - real * sine).astype(jnp.bfloat16).astype(jnp.float32)
            power += eff_real * eff_real + eff_imag * eff_imag
            stage[pl.ds(pl.multiple_of(real_at[j], unit), per_chip), :] = eff_real
            stage[pl.ds(pl.multiple_of(imag_at[j], unit), per_chip), :] = eff_imag
        norm_ref[...] += jnp.sum(power, axis=0, keepdims=True)
        eff1_ref[f] = stage[:split].astype(jnp.bfloat16).T
        eff2_ref[f] = stage[split:].astype(jnp.bfloat16).T


def templates_call(templ_real, templ_imag, channel_mask, moveout, samples, order, early):
    band, channels, templates = templ_real.shape
    chips = order.shape[0]
    per_chip = channels // chips
    half1, half2 = (round_up(n * per_chip, LANES) for n in (early, chips - early))
    depths = [2 * half1, 2 * half2]
    is_early = order < early
    real_at = jnp.where(is_early, order * per_chip, 2 * half1 + (order - early) * per_chip)
    imag_at = real_at + jnp.where(is_early, half1, half2)
    unit = 2.0 * math.pi / samples
    weight = channel_mask.astype(jnp.float32)
    start = (FIRST_BIN * moveout % samples).astype(jnp.float32) * unit
    turn = (moveout % samples).astype(jnp.float32) * unit
    tables = (weight * jnp.cos(start), weight * jnp.sin(start), jnp.cos(turn), jnp.sin(turn))
    step = math.gcd(band, 8)
    full = pl.BlockSpec((channels, templates), lambda i: (0, 0))
    block = pl.BlockSpec((step, channels, templates), lambda i: (i, 0, 0))
    return pl.pallas_call(
        templates_kernel,
        grid=(band // step,),
        in_specs=[pl.BlockSpec(memory_space=pltpu.SMEM)] * 2 + [full] * 4 + [block] * 2,
        out_specs=[pl.BlockSpec((step, templates, d), lambda i: (i, 0, 0)) for d in depths]
        + [pl.BlockSpec((1, templates), lambda i: (0, 0))],
        out_shape=[jax.ShapeDtypeStruct((band, templates, d), jnp.bfloat16) for d in depths]
        + [jax.ShapeDtypeStruct((1, templates), jnp.float32)],
        scratch_shapes=[pltpu.VMEM((channels, templates), jnp.float32)] * 2
        + [pltpu.VMEM((sum(depths), templates), jnp.float32)],
        compiler_params=pltpu.CompilerParams(vmem_limit_bytes=STREAM_LIMIT),
        cost_estimate=cost(12),
        name="templates",
    )(real_at, imag_at, *tables, templ_real, templ_imag)


def inverse_table(samples, band):
    table = jnp.asarray(forward_table(samples, band).T, jnp.float32)
    high = table.astype(jnp.bfloat16)
    low = (table - high.astype(jnp.float32)).astype(jnp.bfloat16)
    return jnp.concatenate([high, high, low], axis=1)


def block_copies(blocks, staged, sems):
    copies = []
    first = 0
    for i, block in enumerate(blocks):
        count = block.shape[0]
        copies.append(pltpu.make_async_copy(block, staged.at[pl.ds(first, count)], sems.at[i]))
        first += count
    return copies


def unpack_blocks(blocks, copies, staged, spec, pitch):
    rows, lanes = staged.shape[1:]
    padded = spec.shape[0] // pitch
    filled = staged.shape[0]

    def clear(c, carry):
        spec[pl.ds(pl.multiple_of(c * pitch, 8), rows), :] = jnp.zeros((rows, lanes), jnp.float32)
        return carry

    lax.fori_loop(filled, padded, clear, 0)
    energy = jnp.zeros((rows, lanes), jnp.float32)
    first = 0
    for block, copy in zip(blocks, copies):
        count = block.shape[0]
        copy.wait()

        def unpack(c, energy):
            value = staged[c].astype(jnp.float32)
            spec[pl.ds(pl.multiple_of(c * pitch, 8), rows), :] = value
            return energy + value * value

        energy = lax.fori_loop(first, first + count, unpack, energy, unroll=math.gcd(count, 10))
        first += count
    return jnp.sum(energy, axis=0, keepdims=True)


def cross_of(packed, eff_a, eff_b, spec, pitch, f, bin_at, band):
    padded = spec.shape[0] // pitch
    lane = lax.broadcasted_iota(jnp.int32, (1, LANES), 1)
    if packed:
        left = spec[pl.ds(bin_at, padded, stride=pitch), :]
        right = jnp.where(lane < HALF, 1.0, -1.0) * pltpu.roll(left, HALF, 1)
        values = jnp.concatenate([left, right], axis=0).astype(jnp.bfloat16)
    else:
        real = spec[pl.ds(bin_at, padded, stride=pitch), :].astype(jnp.bfloat16)
        imag = spec[pl.ds(band + bin_at, padded, stride=pitch), :].astype(jnp.bfloat16)
        top = jnp.concatenate([real, imag], axis=1)
        bottom = jnp.concatenate([imag, -real], axis=1)
        values = jnp.concatenate([top, bottom], axis=0)
    eff = jnp.concatenate([eff_a[f], eff_b[f]], axis=0)
    return jnp.dot(eff, values, preferred_element_type=jnp.float32)


def early_kernel(packed, band, count, *refs):
    blocks = refs[:count]
    eff_a, eff_b, cross_ref, energy_ref, spec, staged, sems = refs[count:]
    rows = blocks[0].shape[1]
    pitch = rows + SKEW
    step = pl.program_id(0)

    @pl.when(step == 0)
    def _():
        copies = block_copies(blocks, staged, sems)
        for copy in copies:
            copy.start()
        energy_ref[...] = unpack_blocks(blocks, copies, staged, spec, pitch)

    bins = eff_a.shape[0]
    for f in range(bins):
        cross_ref[f] = cross_of(packed, eff_a, eff_b, spec, pitch, f, step * bins + f, band)


def late_kernel(packed, band, count, scale, *refs):
    blocks = refs[:count]
    (
        eff_a, eff_b, partial_hbm, energy_in, norm_ref, table_ref, peak_ref, best_ref,
        spec, cross, energy_ref, staged, sems, partial_ref, partial_sems,
    ) = refs[count:]
    rows = blocks[0].shape[1]
    pitch = rows + SKEW
    lanes = LANES
    step = pl.program_id(0)
    bins, templates, _ = eff_a.shape
    group = templates if packed else 2 * templates
    depth = 2 * band
    cross_pitch = depth + SKEW
    lane = lax.broadcasted_iota(jnp.int32, (1, lanes), 1)

    def partial_copy(i):
        here = pl.ds(i * bins, bins)
        return pltpu.make_async_copy(partial_hbm.at[here], partial_ref.at[here], partial_sems.at[i])

    @pl.when(step == 0)
    def _():
        copies = block_copies(blocks, staged, sems)
        for copy in copies:
            copy.start()
        for i in range(partial_ref.shape[0] // bins):
            partial_copy(i).start()
        energy_ref[...] = energy_in[...] + unpack_blocks(blocks, copies, staged, spec, pitch)

    partial_copy(step).wait()

    for f in range(bins):
        at = step * bins + f
        out = partial_ref[at] + cross_of(packed, eff_a, eff_b, spec, pitch, f, at, band)
        if packed:
            first, second = out[:group], out[group:]
            real = jnp.where(lane < HALF, first, pltpu.roll(second, HALF, 1))
            imag = jnp.where(lane < HALF, pltpu.roll(first, HALF, 1), second)
        else:
            real, imag = out[:, :lanes], out[:, lanes:]
        cross[pl.ds(at, group, stride=cross_pitch), :] = real
        cross[pl.ds(band + at, group, stride=cross_pitch), :] = imag

    @pl.when(step == pl.num_programs(0) - 1)
    def _():
        def one_pair(i, carry):
            pair = jnp.concatenate(
                [
                    cross[pl.ds(pl.multiple_of((2 * i + j) * cross_pitch, 8), depth), :]
                    for j in range(2)
                ],
                axis=1,
            )
            high = pair.astype(jnp.bfloat16)
            low = (pair - high.astype(jnp.float32)).astype(jnp.bfloat16)
            values = jnp.concatenate([high, low, high], axis=0)
            out = jnp.dot(table_ref[...], values, preferred_element_type=jnp.float32)
            top = jnp.max(out, axis=0, keepdims=True)
            peak_ref[pl.ds(2 * i, 1), :] = top[:, :lanes]
            peak_ref[pl.ds(2 * i + 1, 1), :] = top[:, lanes:]
            return carry

        lax.fori_loop(0, group // 2, one_pair, 0, unroll=math.gcd(group // 2, 32))
        energy = energy_ref[...]
        norm = norm_ref[...]
        if packed:
            energy = energy + pltpu.roll(energy, HALF, 1)
            templ_norm = jnp.where(lane < HALF, norm[:group], norm[group:])
        else:
            templ_norm = norm
        data_norm = jnp.sqrt(energy + epsilon)
        peak = peak_ref[...] * scale / (templ_norm * data_norm)
        peak_ref[...] = peak
        best = jnp.max(peak, axis=0, keepdims=True)
        if packed:
            best = jnp.maximum(best, pltpu.roll(best, HALF, 1))
        best_ref[...] = best


def whole_block(array):
    return pl.BlockSpec(array.shape, lambda i: (0,) * array.ndim, pipeline_mode=pl.Buffered(1))


def early_call(packed, blocks, eff_a, eff_b):
    band, templates, depth = eff_a.shape
    rows = blocks[0].shape[1]
    step = math.gcd(band, 8)
    wide = LANES if packed else 2 * LANES
    eff_spec = pl.BlockSpec((step, templates, depth), lambda i: (i, 0, 0))
    hbm = pl.BlockSpec(memory_space=pltpu.HBM)
    return pl.pallas_call(
        lambda *refs: early_kernel(packed, band, len(blocks), *refs),
        grid=(band // step,),
        in_specs=[hbm] * len(blocks) + [eff_spec] * 2,
        out_specs=[
            pl.BlockSpec((step, 2 * templates, wide), lambda i: (i, 0, 0)),
            pl.BlockSpec((1, LANES), lambda i: (0, 0)),
        ],
        out_shape=[
            jax.ShapeDtypeStruct((band, 2 * templates, wide), jnp.float32),
            jax.ShapeDtypeStruct((1, LANES), jnp.float32),
        ],
        scratch_shapes=[
            pltpu.VMEM((depth // 2 * (rows + SKEW), LANES), jnp.float32),
            pltpu.VMEM((sum(b.shape[0] for b in blocks), rows, LANES), jnp.bfloat16),
            pltpu.SemaphoreType.DMA((len(blocks),)),
        ],
        compiler_params=pltpu.CompilerParams(vmem_limit_bytes=PACKED_LIMIT if packed else WIDE_LIMIT),
        cost_estimate=cost(10),
        name="early",
    )(*blocks, eff_a, eff_b)


def late_call(packed, blocks, eff_a, eff_b, partial, energy, norm, table, scale):
    band, templates, depth = eff_a.shape
    rows = blocks[0].shape[1]
    step = math.gcd(band, 8)
    group = templates if packed else 2 * templates
    eff_spec = pl.BlockSpec((step, templates, depth), lambda i: (i, 0, 0))
    hbm = pl.BlockSpec(memory_space=pltpu.HBM)
    return pl.pallas_call(
        lambda *refs: late_kernel(packed, band, len(blocks), scale, *refs),
        grid=(band // step,),
        in_specs=[hbm] * len(blocks)
        + [eff_spec] * 2
        + [hbm]
        + [whole_block(a) for a in (energy, norm, table)],
        out_specs=[
            pl.BlockSpec((group, LANES), lambda i: (0, 0)),
            pl.BlockSpec((1, LANES), lambda i: (0, 0)),
        ],
        out_shape=[
            jax.ShapeDtypeStruct((group, LANES), jnp.float32),
            jax.ShapeDtypeStruct((1, LANES), jnp.float32),
        ],
        scratch_shapes=[
            pltpu.VMEM((depth // 2 * (rows + SKEW), LANES), jnp.float32),
            pltpu.VMEM((group * (2 * band + SKEW), LANES), jnp.float32),
            pltpu.VMEM((1, LANES), jnp.float32),
            pltpu.VMEM((sum(b.shape[0] for b in blocks), rows, LANES), jnp.bfloat16),
            pltpu.SemaphoreType.DMA((len(blocks),)),
            pltpu.VMEM(partial.shape, jnp.float32),
            pltpu.SemaphoreType.DMA((band // step,)),
        ],
        compiler_params=pltpu.CompilerParams(vmem_limit_bytes=PACKED_LIMIT if packed else LATE_LIMIT),
        cost_estimate=cost(14),
        name="late",
    )(*blocks, eff_a, eff_b, partial, energy, norm, table)


class Grid:
    def __init__(self, size):
        self.size = size
        self.core = 2
        outer = size // self.core
        self.y = 2 if outer % 2 == 0 else 1
        self.z = outer // self.y

    def place(self, z, y, c):
        return (z * self.y + y) * self.core + c

    @property
    def chips(self):
        return self.z * self.y

    def ring(self):
        turn = [z * self.y for z in range(self.z)]
        if self.y == 2:
            turn += [z * 2 + 1 for z in reversed(range(self.z))]
        return turn

    def ring_pairs(self, sign):
        turn = self.ring()
        return [
            (turn[i] * self.core + c, turn[(i + sign) % len(turn)] * self.core + c)
            for i in range(len(turn))
            for c in range(self.core)
        ]

    def swap_pairs(self):
        return [(i, i ^ 1) for i in range(self.size)]

    def z_pairs(self, distance):
        return [
            (self.place(z, y, c), self.place(z ^ distance, y, c))
            for z in range(self.z)
            for y in range(self.y)
            for c in range(self.core)
        ]

    def y_pairs(self):
        return [
            (self.place(z, y, c), self.place(z, 1 - y, c))
            for z in range(self.z)
            for y in range(self.y)
            for c in range(self.core)
        ]


def body(raw_trace, fir_taps, templ_real, templ_imag, channel_mask, moveout, *, row):
    grid = Grid(row)
    chips = grid.chips
    local_channels, windows, raw_length = raw_trace.shape
    samples = raw_length // 2
    band, channels, local_templates = templ_real.shape
    wide = windows // 2 // LANES * LANES
    index = lax.axis_index("row")
    core = index % grid.core
    first = core == 0

    def swap(value):
        return lax.ppermute(value, "row", grid.swap_pairs())

    def chip_block(keep, got):
        return jnp.stack([jnp.where(first, keep, got), jnp.where(first, got, keep)])

    core_table = core[None].astype(jnp.int32)
    p_keep, p_send = spectra_call(False, raw_trace, fir_taps, core_table, band)
    p_own = chip_block(p_keep, swap(p_send))
    turn = np.asarray(grid.ring())
    arrival = [0]
    for s in range(1, (chips - 1) // 2 + 1):
        arrival += [-s, s]
    if chips % 2 == 0:
        arrival.append(chips // 2)
    last_step = chips // 2
    early_steps = chips // 4
    early = 1 + 2 * early_steps
    rank = np.zeros((chips, chips), np.int32)
    for i in range(chips):
        for k, away in enumerate(arrival):
            rank[turn[i], turn[(i + away) % chips]] = k
    order = jnp.asarray(rank)[index // grid.core]

    raw_trace, templ_real, templ_imag, channel_mask, moveout, p_own = lax.optimization_barrier(
        (raw_trace, templ_real, templ_imag, channel_mask, moveout, p_own)
    )
    q_keep, q_send = spectra_call(True, raw_trace, fir_taps, core_table, band)
    eff1, eff2, norm = templates_call(
        templ_real, templ_imag, channel_mask, moveout, samples, order, early
    )
    table = inverse_table(samples, band)
    scale = math.sqrt(2.0 * channels * band)

    def forth(value):
        return lax.ppermute(value, "row", grid.ring_pairs(1))

    def back(value):
        return lax.ppermute(value, "row", grid.ring_pairs(-1))

    def flat(block):
        return block.reshape((-1,) + block.shape[-2:])

    def step(up, down, s):
        if 2 * s == chips:
            return forth(up[0]), back(down[1])
        return forth(up), back(down)

    def early_part(packed, blocks):
        return early_call(packed, [flat(b) for b in blocks], eff1, eff1_other)

    def late_part(packed, blocks, partial, energy):
        return late_call(
            packed, [flat(b) for b in blocks], eff2, eff2_other, partial, energy, templ_norm, table, scale
        )

    tie = lax.optimization_barrier
    p_blocks, q_blocks = [p_own], []
    p_up = p_down = p_own
    for s in range(1, last_step + 1):
        if s == last_step:
            p_early = early_part(False, p_blocks[:early])
            p_up, p_down, q_up, q_down, p_early = tie((p_up, p_down, q_up, q_down, p_early))
        p_up, p_down = step(p_up, p_down, s)
        p_blocks += [p_up, p_down]
        if s == 1:
            q_keep, q_send, p_up, p_down = tie((q_keep, q_send, p_up, p_down))
            q_own = chip_block(q_keep, swap(q_send))
            q_blocks.append(q_own)
            q_up = q_down = q_own
        elif s < last_step:
            q_up, q_down = step(q_up, q_down, s - 1)
            q_blocks += [q_up, q_down]
        if s == 2:
            eff1, eff2, norm, p_up, p_down, q_up, q_down = tie(
                (eff1, eff2, norm, p_up, p_down, q_up, q_down)
            )
            eff1_other, eff2_other = swap(eff1), swap(eff2)
            norm_pair = jnp.stack([norm[0], swap(norm)[0]])
            templ_norm = jnp.sqrt(norm_pair + epsilon).reshape(2 * local_templates, 1)
    q_up, q_down = step(q_up, q_down, last_step - 1)
    q_early = early_part(True, q_blocks[:early])
    p_up, p_down, q_up, q_down, q_early = tie((p_up, p_down, q_up, q_down, q_early))
    p_blocks[-2:] = [p_up, p_down]
    q_blocks += [q_up, q_down]
    q_blocks += step(q_up, q_down, last_step)
    p_peak, p_best = late_part(False, p_blocks[early:], *p_early)
    q_peak, q_best = late_part(True, q_blocks[early:], *q_early)

    p_other = swap(p_peak[local_templates:])
    q_other = swap(q_peak[:, HALF:])
    q_mine = q_peak[:, :HALF]
    p_mine = p_peak[:local_templates]
    peak = jnp.concatenate(
        [
            jnp.where(first, p_mine, p_other),
            jnp.where(first, p_other, p_mine),
            jnp.where(first, q_mine, q_other),
            jnp.where(first, q_other, q_mine),
        ],
        axis=1,
    )

    mine = jnp.concatenate([p_best, q_best], axis=1)
    if grid.y == 2:
        mine = jnp.maximum(mine, lax.ppermute(mine, "row", grid.y_pairs()))
    if grid.z & (grid.z - 1) == 0:
        distance = 1
        while distance < grid.z:
            mine = jnp.maximum(mine, lax.ppermute(mine, "row", grid.z_pairs(distance)))
            distance *= 2
    else:
        mine = lax.pmax(mine, "row")
    mine, peak = tie((mine, peak))
    other = swap(mine)
    one = jnp.where(first, mine, other)[0]
    two = jnp.where(first, other, mine)[0]
    best = jnp.concatenate(
        [one[:wide], two[:wide], one[wide : wide + HALF], two[wide : wide + HALF]]
    )
    return (peak, best)


def solution(mesh):
    in_specs = (
        P("row", "parts", None),
        P(),
        P(None, None, "row"),
        P(None, None, "row"),
        P(None, "row"),
        P(None, "row"),
    )
    out_specs = (P("row", "parts"), P("parts"))
    row = mesh.shape["row"]

    def local(*args):
        return body(*args, row=row)

    return jax.shard_map(local, mesh=mesh, in_specs=in_specs, out_specs=out_specs, check_vma=False)
```

```python
import math

import jax
import jax.numpy as jnp
import numpy as np
from jax import lax
from jax.experimental import pallas as pl
from jax.experimental.pallas import tpu as pltpu
from jax.sharding import PartitionSpec as P

FIRST_BIN = 16
LANES = 128
HALF = LANES // 2
SKEW = 8
WIDE_LIMIT = 31 * 2**20
PACKED_LIMIT = 19 * 2**20
LATE_LIMIT = 40 * 2**20
STREAM_LIMIT = 56 * 2**20

epsilon = 1e-06


def cost(microseconds):
    return pl.CostEstimate(flops=0, bytes_accessed=int(microseconds * 3e6), transcendentals=0)


def split_three(wide):
    high = wide.astype(jnp.bfloat16)
    rest = wide - high.astype(jnp.float32)
    middle = rest.astype(jnp.bfloat16)
    low = (rest - middle.astype(jnp.float32)).astype(jnp.bfloat16)
    return high, middle, low


def forward_table(samples, band):
    turns = (np.arange(samples)[None, :] * (FIRST_BIN + np.arange(band))[:, None]) % samples
    angles = 2.0 * np.pi / samples * turns
    return np.concatenate([np.cos(angles), -np.sin(angles)], axis=0)


def spectra_kernel(packed, band, core_ref, fir_ref, table_ref, x_ref, keep_ref, send_ref, w_ref):
    count, windows, raw_length = x_ref.shape
    samples = raw_length // 2
    taps = fir_ref.shape[0]
    rows = 2 * band

    @pl.when(pl.program_id(0) == 0)
    def _():
        lane = lax.broadcasted_iota(jnp.int32, (8, raw_length), 1)
        base = jnp.zeros((8, raw_length), jnp.float32)
        for k in range(taps):
            base = jnp.where(lane == (raw_length - k) % raw_length, fir_ref[k], base)
        turned = pltpu.roll(
            jnp.concatenate([base] * (samples // 8), axis=0), 0, 1, stride=2, stride_axis=0
        )
        n = lax.broadcasted_iota(jnp.int32, (samples, raw_length), 0)
        m = lax.broadcasted_iota(jnp.int32, (samples, raw_length), 1)
        filt = jnp.where(m <= 2 * n, turned, 0.0)
        combined = jnp.dot(
            table_ref[...], filt, precision=lax.Precision.HIGHEST, preferred_element_type=jnp.float32
        )
        high, middle, low = (piece.astype(jnp.float32) for piece in split_three(combined))
        none = jnp.zeros_like(high)
        for i, pair in enumerate(((high, middle), (low, none), (high, none))):
            turned_pair = jnp.concatenate(pair, axis=0).T.astype(jnp.bfloat16)
            w_ref[:, 2 * i * rows : 2 * (i + 1) * rows] = turned_pair

    first = core_ref[0] == 0
    lane = lax.broadcasted_iota(jnp.int32, (band, LANES), 1)
    for c in range(count):
        high, middle, low = split_three(x_ref[c])
        one = jnp.dot(high, w_ref[:, : 4 * rows], preferred_element_type=jnp.float32)
        two = jnp.dot(middle, w_ref[:, : 2 * rows], preferred_element_type=jnp.float32)
        three = jnp.dot(low, w_ref[:, 4 * rows :], preferred_element_type=jnp.float32)
        total = (((one[:, 2 * rows :] + three) + two) + one[:, : 2 * rows]).T
        out = total[:rows] + total[rows:]
        if packed:
            real, imag = out[:band], out[band:]
            left = jnp.where(lane < HALF, real, pltpu.roll(imag, HALF, 1))
            right = jnp.where(lane < HALF, pltpu.roll(real, HALF, 1), imag)
        else:
            left, right = out[:, : windows // 2], out[:, windows // 2 :]
        keep_ref[c] = jnp.where(first, left, right).astype(jnp.bfloat16)
        send_ref[c] = jnp.where(first, right, left).astype(jnp.bfloat16)


def spectra_call(packed, raw_trace, fir_taps, core, band):
    channels, windows, raw_length = raw_trace.shape
    samples = raw_length // 2
    step = math.gcd(channels, 10)
    wide = windows - LANES
    table = jnp.asarray(forward_table(samples, band), jnp.float32)
    shape = (channels, band, LANES) if packed else (channels, 2 * band, wide // 2)
    taken = (step, LANES if packed else wide, raw_length)
    at = wide // LANES if packed else 0
    smem = pl.BlockSpec(memory_space=pltpu.SMEM)
    out_block = pl.BlockSpec((step,) + shape[1:], lambda i: (i, 0, 0))
    return pl.pallas_call(
        lambda *refs: spectra_kernel(packed, band, *refs),
        grid=(channels // step,),
        in_specs=[
            smem,
            smem,
            pl.BlockSpec(table.shape, lambda i: (0, 0)),
            pl.BlockSpec(taken, lambda i: (i, at, 0)),
        ],
        out_specs=[out_block] * 2,
        out_shape=[jax.ShapeDtypeStruct(shape, jnp.bfloat16)] * 2,
        scratch_shapes=[pltpu.VMEM((raw_length, 12 * band), jnp.bfloat16)],
        compiler_params=pltpu.CompilerParams(vmem_limit_bytes=STREAM_LIMIT),
        cost_estimate=cost(5 if packed else 8),
        name="spectra",
    )(core, fir_taps, table, raw_trace)


def round_up(value, unit):
    return -(-value // unit) * unit


def templates_kernel(
    real_at, imag_at, cos0, sin0, cos1, sin1, real_ref, imag_ref,
    eff1_ref, eff2_ref, norm_ref, cos_ref, sin_ref, stage,
):
    bins, channels, templates = real_ref.shape
    chips = real_at.shape[0]
    per_chip = channels // chips
    unit = math.gcd(per_chip, 8)
    split = eff1_ref.shape[2]

    @pl.when(pl.program_id(0) == 0)
    def _():
        cos_ref[...] = cos0[...]
        sin_ref[...] = sin0[...]
        norm_ref[...] = jnp.zeros_like(norm_ref)
        stage[...] = jnp.zeros_like(stage)

    for f in range(bins):
        power = jnp.zeros((per_chip, templates), jnp.float32)
        for j in range(chips):
            here = pl.ds(j * per_chip, per_chip)
            cosine, sine = cos_ref[here, :], sin_ref[here, :]
            cos_ref[here, :] = cosine * cos1[here, :] - sine * sin1[here, :]
            sin_ref[here, :] = sine * cos1[here, :] + cosine * sin1[here, :]
            real = real_ref[f, here, :].astype(jnp.float32)
            imag = imag_ref[f, here, :].astype(jnp.float32)
            eff_real = (real * cosine + imag * sine).astype(jnp.bfloat16).astype(jnp.float32)
            eff_imag = (imag * cosine - real * sine).astype(jnp.bfloat16).astype(jnp.float32)
            power += eff_real * eff_real + eff_imag * eff_imag
            stage[pl.ds(pl.multiple_of(real_at[j], unit), per_chip), :] = eff_real
            stage[pl.ds(pl.multiple_of(imag_at[j], unit), per_chip), :] = eff_imag
        norm_ref[...] += jnp.sum(power, axis=0, keepdims=True)
        eff1_ref[f] = stage[:split].astype(jnp.bfloat16).T
        eff2_ref[f] = stage[split:].astype(jnp.bfloat16).T


def templates_call(templ_real, templ_imag, channel_mask, moveout, samples, order, early):
    band, channels, templates = templ_real.shape
    chips = order.shape[0]
    per_chip = channels // chips
    half1, half2 = (round_up(n * per_chip, LANES) for n in (early, chips - early))
    depths = [2 * half1, 2 * half2]
    is_early = order < early
    real_at = jnp.where(is_early, order * per_chip, 2 * half1 + (order - early) * per_chip)
    imag_at = real_at + jnp.where(is_early, half1, half2)
    unit = 2.0 * math.pi / samples
    weight = channel_mask.astype(jnp.float32)
    start = (FIRST_BIN * moveout % samples).astype(jnp.float32) * unit
    turn = (moveout % samples).astype(jnp.float32) * unit
    tables = (weight * jnp.cos(start), weight * jnp.sin(start), jnp.cos(turn), jnp.sin(turn))
    step = math.gcd(band, 8)
    full = pl.BlockSpec((channels, templates), lambda i: (0, 0))
    block = pl.BlockSpec((step, channels, templates), lambda i: (i, 0, 0))
    return pl.pallas_call(
        templates_kernel,
        grid=(band // step,),
        in_specs=[pl.BlockSpec(memory_space=pltpu.SMEM)] * 2 + [full] * 4 + [block] * 2,
        out_specs=[pl.BlockSpec((step, templates, d), lambda i: (i, 0, 0)) for d in depths]
        + [pl.BlockSpec((1, templates), lambda i: (0, 0))],
        out_shape=[jax.ShapeDtypeStruct((band, templates, d), jnp.bfloat16) for d in depths]
        + [jax.ShapeDtypeStruct((1, templates), jnp.float32)],
        scratch_shapes=[pltpu.VMEM((channels, templates), jnp.float32)] * 2
        + [pltpu.VMEM((sum(depths), templates), jnp.float32)],
        compiler_params=pltpu.CompilerParams(vmem_limit_bytes=STREAM_LIMIT),
        cost_estimate=cost(12),
        name="templates",
    )(real_at, imag_at, *tables, templ_real, templ_imag)


def inverse_table(samples, band):
    table = jnp.asarray(forward_table(samples, band).T, jnp.float32)
    high = table.astype(jnp.bfloat16)
    low = (table - high.astype(jnp.float32)).astype(jnp.bfloat16)
    return jnp.concatenate([high, high, low], axis=1)


def block_copies(blocks, staged, sems):
    copies = []
    first = 0
    for i, block in enumerate(blocks):
        count = block.shape[0]
        copies.append(pltpu.make_async_copy(block, staged.at[pl.ds(first, count)], sems.at[i]))
        first += count
    return copies


def unpack_blocks(blocks, copies, staged, spec, pitch):
    rows, lanes = staged.shape[1:]
    padded = spec.shape[0] // pitch
    filled = staged.shape[0]

    def clear(c, carry):
        spec[pl.ds(pl.multiple_of(c * pitch, 8), rows), :] = jnp.zeros((rows, lanes), jnp.float32)
        return carry

    lax.fori_loop(filled, padded, clear, 0)
    energy = jnp.zeros((rows, lanes), jnp.float32)
    first = 0
    for block, copy in zip(blocks, copies):
        count = block.shape[0]
        copy.wait()

        def unpack(c, energy):
            value = staged[c].astype(jnp.float32)
            spec[pl.ds(pl.multiple_of(c * pitch, 8), rows), :] = value
            return energy + value * value

        energy = lax.fori_loop(first, first + count, unpack, energy, unroll=math.gcd(count, 10))
        first += count
    return jnp.sum(energy, axis=0, keepdims=True)


def cross_of(packed, eff_a, eff_b, spec, pitch, f, bin_at, band):
    padded = spec.shape[0] // pitch
    lane = lax.broadcasted_iota(jnp.int32, (1, LANES), 1)
    if packed:
        left = spec[pl.ds(bin_at, padded, stride=pitch), :]
        right = jnp.where(lane < HALF, 1.0, -1.0) * pltpu.roll(left, HALF, 1)
        values = jnp.concatenate([left, right], axis=0).astype(jnp.bfloat16)
    else:
        real = spec[pl.ds(bin_at, padded, stride=pitch), :].astype(jnp.bfloat16)
        imag = spec[pl.ds(band + bin_at, padded, stride=pitch), :].astype(jnp.bfloat16)
        top = jnp.concatenate([real, imag], axis=1)
        bottom = jnp.concatenate([imag, -real], axis=1)
        values = jnp.concatenate([top, bottom], axis=0)
    eff = jnp.concatenate([eff_a[f], eff_b[f]], axis=0)
    return jnp.dot(eff, values, preferred_element_type=jnp.float32)


def early_kernel(packed, band, count, *refs):
    blocks = refs[:count]
    eff_a, eff_b, cross_ref, energy_ref, spec, staged, sems = refs[count:]
    rows = blocks[0].shape[1]
    pitch = rows + SKEW
    step = pl.program_id(0)

    @pl.when(step == 0)
    def _():
        copies = block_copies(blocks, staged, sems)
        for copy in copies:
            copy.start()
        energy_ref[...] = unpack_blocks(blocks, copies, staged, spec, pitch)

    bins = eff_a.shape[0]
    for f in range(bins):
        cross_ref[f] = cross_of(packed, eff_a, eff_b, spec, pitch, f, step * bins + f, band)


def late_kernel(packed, band, count, scale, *refs):
    blocks = refs[:count]
    (
        eff_a, eff_b, partial_hbm, energy_in, norm_ref, table_ref, peak_ref, best_ref,
        spec, cross, energy_ref, staged, sems, partial_ref, partial_sems,
    ) = refs[count:]
    rows = blocks[0].shape[1]
    pitch = rows + SKEW
    lanes = LANES
    step = pl.program_id(0)
    bins, templates, _ = eff_a.shape
    group = templates if packed else 2 * templates
    depth = 2 * band
    cross_pitch = depth + SKEW
    lane = lax.broadcasted_iota(jnp.int32, (1, lanes), 1)

    def partial_copy(i):
        here = pl.ds(i * bins, bins)
        return pltpu.make_async_copy(partial_hbm.at[here], partial_ref.at[here], partial_sems.at[i])

    @pl.when(step == 0)
    def _():
        copies = block_copies(blocks, staged, sems)
        for copy in copies:
            copy.start()
        for i in range(partial_ref.shape[0] // bins):
            partial_copy(i).start()
        energy_ref[...] = energy_in[...] + unpack_blocks(blocks, copies, staged, spec, pitch)

    partial_copy(step).wait()

    for f in range(bins):
        at = step * bins + f
        out = partial_ref[at] + cross_of(packed, eff_a, eff_b, spec, pitch, f, at, band)
        if packed:
            first, second = out[:group], out[group:]
            real = jnp.where(lane < HALF, first, pltpu.roll(second, HALF, 1))
            imag = jnp.where(lane < HALF, pltpu.roll(first, HALF, 1), second)
        else:
            real, imag = out[:, :lanes], out[:, lanes:]
        cross[pl.ds(at, group, stride=cross_pitch), :] = real
        cross[pl.ds(band + at, group, stride=cross_pitch), :] = imag

    @pl.when(step == pl.num_programs(0) - 1)
    def _():
        def one_pair(i, carry):
            pair = jnp.concatenate(
                [
                    cross[pl.ds(pl.multiple_of((2 * i + j) * cross_pitch, 8), depth), :]
                    for j in range(2)
                ],
                axis=1,
            )
            high = pair.astype(jnp.bfloat16)
            low = (pair - high.astype(jnp.float32)).astype(jnp.bfloat16)
            values = jnp.concatenate([high, low, high], axis=0)
            out = jnp.dot(table_ref[...], values, preferred_element_type=jnp.float32)
            top = jnp.max(out, axis=0, keepdims=True)
            peak_ref[pl.ds(2 * i, 1), :] = top[:, :lanes]
            peak_ref[pl.ds(2 * i + 1, 1), :] = top[:, lanes:]
            return carry

        lax.fori_loop(0, group // 2, one_pair, 0, unroll=math.gcd(group // 2, 32))
        energy = energy_ref[...]
        norm = norm_ref[...]
        if packed:
            energy = energy + pltpu.roll(energy, HALF, 1)
            templ_norm = jnp.where(lane < HALF, norm[:group], norm[group:])
        else:
            templ_norm = norm
        data_norm = jnp.sqrt(energy + epsilon)
        peak = peak_ref[...] * scale / (templ_norm * data_norm)
        peak_ref[...] = peak
        best = jnp.max(peak, axis=0, keepdims=True)
        if packed:
            best = jnp.maximum(best, pltpu.roll(best, HALF, 1))
        best_ref[...] = best


def whole_block(array):
    return pl.BlockSpec(array.shape, lambda i: (0,) * array.ndim, pipeline_mode=pl.Buffered(1))


def early_call(packed, blocks, eff_a, eff_b):
    band, templates, depth = eff_a.shape
    rows = blocks[0].shape[1]
    step = math.gcd(band, 8)
    wide = LANES if packed else 2 * LANES
    eff_spec = pl.BlockSpec((step, templates, depth), lambda i: (i, 0, 0))
    hbm = pl.BlockSpec(memory_space=pltpu.HBM)
    return pl.pallas_call(
        lambda *refs: early_kernel(packed, band, len(blocks), *refs),
        grid=(band // step,),
        in_specs=[hbm] * len(blocks) + [eff_spec] * 2,
        out_specs=[
            pl.BlockSpec((step, 2 * templates, wide), lambda i: (i, 0, 0)),
            pl.BlockSpec((1, LANES), lambda i: (0, 0)),
        ],
        out_shape=[
            jax.ShapeDtypeStruct((band, 2 * templates, wide), jnp.float32),
            jax.ShapeDtypeStruct((1, LANES), jnp.float32),
        ],
        scratch_shapes=[
            pltpu.VMEM((depth // 2 * (rows + SKEW), LANES), jnp.float32),
            pltpu.VMEM((sum(b.shape[0] for b in blocks), rows, LANES), jnp.bfloat16),
            pltpu.SemaphoreType.DMA((len(blocks),)),
        ],
        compiler_params=pltpu.CompilerParams(vmem_limit_bytes=PACKED_LIMIT if packed else WIDE_LIMIT),
        cost_estimate=cost(10),
        name="early",
    )(*blocks, eff_a, eff_b)


def late_call(packed, blocks, eff_a, eff_b, partial, energy, norm, table, scale):
    band, templates, depth = eff_a.shape
    rows = blocks[0].shape[1]
    step = math.gcd(band, 8)
    group = templates if packed else 2 * templates
    eff_spec = pl.BlockSpec((step, templates, depth), lambda i: (i, 0, 0))
    hbm = pl.BlockSpec(memory_space=pltpu.HBM)
    return pl.pallas_call(
        lambda *refs: late_kernel(packed, band, len(blocks), scale, *refs),
        grid=(band // step,),
        in_specs=[hbm] * len(blocks)
        + [eff_spec] * 2
        + [hbm]
        + [whole_block(a) for a in (energy, norm, table)],
        out_specs=[
            pl.BlockSpec((group, LANES), lambda i: (0, 0)),
            pl.BlockSpec((1, LANES), lambda i: (0, 0)),
        ],
        out_shape=[
            jax.ShapeDtypeStruct((group, LANES), jnp.float32),
            jax.ShapeDtypeStruct((1, LANES), jnp.float32),
        ],
        scratch_shapes=[
            pltpu.VMEM((depth // 2 * (rows + SKEW), LANES), jnp.float32),
            pltpu.VMEM((group * (2 * band + SKEW), LANES), jnp.float32),
            pltpu.VMEM((1, LANES), jnp.float32),
            pltpu.VMEM((sum(b.shape[0] for b in blocks), rows, LANES), jnp.bfloat16),
            pltpu.SemaphoreType.DMA((len(blocks),)),
            pltpu.VMEM(partial.shape, jnp.float32),
            pltpu.SemaphoreType.DMA((band // step,)),
        ],
        compiler_params=pltpu.CompilerParams(vmem_limit_bytes=PACKED_LIMIT if packed else LATE_LIMIT),
        cost_estimate=cost(14),
        name="late",
    )(*blocks, eff_a, eff_b, partial, energy, norm, table)


class Grid:
    def __init__(self, size):
        self.size = size
        self.core = 2
        outer = size // self.core
        self.y = 2 if outer % 2 == 0 else 1
        self.z = outer // self.y

    def place(self, z, y, c):
        return (z * self.y + y) * self.core + c

    @property
    def chips(self):
        return self.z * self.y

    def ring(self):
        turn = [z * self.y for z in range(self.z)]
        if self.y == 2:
            turn += [z * 2 + 1 for z in reversed(range(self.z))]
        return turn

    def ring_pairs(self, sign):
        turn = self.ring()
        return [
            (turn[i] * self.core + c, turn[(i + sign) % len(turn)] * self.core + c)
            for i in range(len(turn))
            for c in range(self.core)
        ]

    def swap_pairs(self):
        return [(i, i ^ 1) for i in range(self.size)]

    def z_pairs(self, distance):
        return [
            (self.place(z, y, c), self.place(z ^ distance, y, c))
            for z in range(self.z)
            for y in range(self.y)
            for c in range(self.core)
        ]

    def square_pairs(self):
        return [
            (self.place(z, y, c), self.place(z ^ 1, 1 - y, c))
            for z in range(self.z)
            for y in range(self.y)
            for c in range(self.core)
        ]

    def y_pairs(self):
        return [
            (self.place(z, y, c), self.place(z, 1 - y, c))
            for z in range(self.z)
            for y in range(self.y)
            for c in range(self.core)
        ]


def body(raw_trace, fir_taps, templ_real, templ_imag, channel_mask, moveout, *, row):
    grid = Grid(row)
    chips = grid.chips
    local_channels, windows, raw_length = raw_trace.shape
    samples = raw_length // 2
    band, channels, local_templates = templ_real.shape
    wide = windows // 2 // LANES * LANES
    index = lax.axis_index("row")
    core = index % grid.core
    first = core == 0

    def swap(value):
        return lax.ppermute(value, "row", grid.swap_pairs())

    def chip_block(keep, got):
        return jnp.stack([jnp.where(first, keep, got), jnp.where(first, got, keep)])

    core_table = core[None].astype(jnp.int32)
    p_keep, p_send = spectra_call(False, raw_trace, fir_taps, core_table, band)
    p_own = chip_block(p_keep, swap(p_send))
    turn = np.asarray(grid.ring())
    arrival = [0]
    for s in range(1, (chips - 1) // 2 + 1):
        arrival += [-s, s]
    if chips % 2 == 0:
        arrival.append(chips // 2)
    last_step = chips // 2
    early_steps = chips // 4
    early = 1 + 2 * early_steps
    rank = np.zeros((chips, chips), np.int32)
    for i in range(chips):
        for k, away in enumerate(arrival):
            rank[turn[i], turn[(i + away) % chips]] = k
    order = jnp.asarray(rank)[index // grid.core]

    raw_trace, templ_real, templ_imag, channel_mask, moveout, p_own = lax.optimization_barrier(
        (raw_trace, templ_real, templ_imag, channel_mask, moveout, p_own)
    )
    q_keep, q_send = spectra_call(True, raw_trace, fir_taps, core_table, band)
    eff1, eff2, norm = templates_call(
        templ_real, templ_imag, channel_mask, moveout, samples, order, early
    )
    table = inverse_table(samples, band)
    scale = math.sqrt(2.0 * channels * band)

    def forth(value):
        return lax.ppermute(value, "row", grid.ring_pairs(1))

    def back(value):
        return lax.ppermute(value, "row", grid.ring_pairs(-1))

    def flat(block):
        return block.reshape((-1,) + block.shape[-2:])

    def step(up, down, s):
        if 2 * s == chips:
            return forth(up[0]), back(down[1])
        return forth(up), back(down)

    def early_part(packed, blocks):
        return early_call(packed, [flat(b) for b in blocks], eff1, eff1_other)

    def late_part(packed, blocks, partial, energy):
        return late_call(
            packed, [flat(b) for b in blocks], eff2, eff2_other, partial, energy, templ_norm, table, scale
        )

    tie = lax.optimization_barrier
    p_blocks, q_blocks = [p_own], []
    p_up = p_down = p_own
    for s in range(1, last_step + 1):
        if s == last_step:
            p_early = early_part(False, p_blocks[:early])
            p_up, p_down, q_up, q_down, p_early = tie((p_up, p_down, q_up, q_down, p_early))
        p_up, p_down = step(p_up, p_down, s)
        p_blocks += [p_up, p_down]
        if s == 1:
            q_keep, q_send, p_up, p_down = tie((q_keep, q_send, p_up, p_down))
            q_own = chip_block(q_keep, swap(q_send))
            q_blocks.append(q_own)
            q_up = q_down = q_own
        elif s < last_step:
            q_up, q_down = step(q_up, q_down, s - 1)
            q_blocks += [q_up, q_down]
        if s == 2:
            eff1, eff2, norm, p_up, p_down, q_up, q_down = tie(
                (eff1, eff2, norm, p_up, p_down, q_up, q_down)
            )
            eff1_other, eff2_other = swap(eff1), swap(eff2)
            norm_pair = jnp.stack([norm[0], swap(norm)[0]])
            templ_norm = jnp.sqrt(norm_pair + epsilon).reshape(2 * local_templates, 1)
    q_up, q_down = step(q_up, q_down, last_step - 1)
    q_early = early_part(True, q_blocks[:early])
    p_up, p_down, q_up, q_down, q_early = tie((p_up, p_down, q_up, q_down, q_early))
    p_blocks[-2:] = [p_up, p_down]
    q_blocks += [q_up, q_down]
    q_blocks += step(q_up, q_down, last_step)
    p_peak, p_best = late_part(False, p_blocks[early:], *p_early)
    q_peak, q_best = late_part(True, q_blocks[early:], *q_early)

    p_other = swap(p_peak[local_templates:])
    q_other = swap(q_peak[:, HALF:])
    q_mine = q_peak[:, :HALF]
    p_mine = p_peak[:local_templates]
    peak = jnp.concatenate(
        [
            jnp.where(first, p_mine, p_other),
            jnp.where(first, p_other, p_mine),
            jnp.where(first, q_mine, q_other),
            jnp.where(first, q_other, q_mine),
        ],
        axis=1,
    )

    mine = jnp.concatenate([p_best, q_best], axis=1)
    distance = 1
    if grid.y == 2 and grid.z % 2 == 0:
        others = [grid.y_pairs(), grid.z_pairs(1), grid.square_pairs()]
        for got in [lax.ppermute(mine, "row", pairs) for pairs in others]:
            mine = jnp.maximum(mine, got)
        distance = 2
    elif grid.y == 2:
        mine = jnp.maximum(mine, lax.ppermute(mine, "row", grid.y_pairs()))
    if grid.z & (grid.z - 1) == 0:
        while distance < grid.z:
            mine = jnp.maximum(mine, lax.ppermute(mine, "row", grid.z_pairs(distance)))
            distance *= 2
    else:
        mine = lax.pmax(mine, "row")
    mine, peak = tie((mine, peak))
    other = swap(mine)
    one = jnp.where(first, mine, other)[0]
    two = jnp.where(first, other, mine)[0]
    best = jnp.concatenate(
        [one[:wide], two[:wide], one[wide : wide + HALF], two[wide : wide + HALF]]
    )
    return (peak, best)


def solution(mesh):
    in_specs = (
        P("row", "parts", None),
        P(),
        P(None, None, "row"),
        P(None, None, "row"),
        P(None, "row"),
        P(None, "row"),
    )
    out_specs = (P("row", "parts"), P("parts"))
    row = mesh.shape["row"]

    def local(*args):
        return body(*args, row=row)

    return jax.shard_map(local, mesh=mesh, in_specs=in_specs, out_specs=out_specs, check_vma=False)
```

```python
import math

import jax
import jax.numpy as jnp
import numpy as np
from jax import lax
from jax.experimental import pallas as pl
from jax.experimental.pallas import tpu as pltpu
from jax.sharding import PartitionSpec as P

FIRST_BIN = 16
LANES = 128
HALF = LANES // 2
SKEW = 8
WIDE_LIMIT = 31 * 2**20
PACKED_LIMIT = 19 * 2**20
LATE_LIMIT = 40 * 2**20
STREAM_LIMIT = 56 * 2**20

epsilon = 1e-06


def cost(microseconds):
    return pl.CostEstimate(flops=0, bytes_accessed=int(microseconds * 3e6), transcendentals=0)


def split_three(wide):
    high = wide.astype(jnp.bfloat16)
    rest = wide - high.astype(jnp.float32)
    middle = rest.astype(jnp.bfloat16)
    low = (rest - middle.astype(jnp.float32)).astype(jnp.bfloat16)
    return high, middle, low


def forward_table(samples, band):
    turns = (np.arange(samples)[None, :] * (FIRST_BIN + np.arange(band))[:, None]) % samples
    angles = 2.0 * np.pi / samples * turns
    return np.concatenate([np.cos(angles), -np.sin(angles)], axis=0)


def spectra_kernel(packed, band, core_ref, fir_ref, table_ref, x_ref, keep_ref, send_ref, w_ref):
    count, windows, raw_length = x_ref.shape
    samples = raw_length // 2
    taps = fir_ref.shape[0]
    rows = 2 * band

    @pl.when(pl.program_id(0) == 0)
    def _():
        lane = lax.broadcasted_iota(jnp.int32, (8, raw_length), 1)
        base = jnp.zeros((8, raw_length), jnp.float32)
        for k in range(taps):
            base = jnp.where(lane == (raw_length - k) % raw_length, fir_ref[k], base)
        turned = pltpu.roll(
            jnp.concatenate([base] * (samples // 8), axis=0), 0, 1, stride=2, stride_axis=0
        )
        n = lax.broadcasted_iota(jnp.int32, (samples, raw_length), 0)
        m = lax.broadcasted_iota(jnp.int32, (samples, raw_length), 1)
        filt = jnp.where(m <= 2 * n, turned, 0.0)
        combined = jnp.dot(
            table_ref[...], filt, precision=lax.Precision.HIGHEST, preferred_element_type=jnp.float32
        )
        high, middle, low = (piece.astype(jnp.float32) for piece in split_three(combined))
        none = jnp.zeros_like(high)
        for i, pair in enumerate(((high, middle), (low, none), (high, none))):
            turned_pair = jnp.concatenate(pair, axis=0).T.astype(jnp.bfloat16)
            w_ref[:, 2 * i * rows : 2 * (i + 1) * rows] = turned_pair

    first = core_ref[0] == 0
    lane = lax.broadcasted_iota(jnp.int32, (band, LANES), 1)
    for c in range(count):
        high, middle, low = split_three(x_ref[c])
        one = jnp.dot(high, w_ref[:, : 4 * rows], preferred_element_type=jnp.float32)
        two = jnp.dot(middle, w_ref[:, : 2 * rows], preferred_element_type=jnp.float32)
        three = jnp.dot(low, w_ref[:, 4 * rows :], preferred_element_type=jnp.float32)
        total = (((one[:, 2 * rows :] + three) + two) + one[:, : 2 * rows]).T
        out = total[:rows] + total[rows:]
        if packed:
            real, imag = out[:band], out[band:]
            left = jnp.where(lane < HALF, real, pltpu.roll(imag, HALF, 1))
            right = jnp.where(lane < HALF, pltpu.roll(real, HALF, 1), imag)
        else:
            left, right = out[:, : windows // 2], out[:, windows // 2 :]
        keep_ref[c] = jnp.where(first, left, right).astype(jnp.bfloat16)
        send_ref[c] = jnp.where(first, right, left).astype(jnp.bfloat16)


def spectra_call(packed, raw_trace, fir_taps, core, band):
    channels, windows, raw_length = raw_trace.shape
    samples = raw_length // 2
    step = math.gcd(channels, 10)
    wide = windows - LANES
    table = jnp.asarray(forward_table(samples, band), jnp.float32)
    shape = (channels, band, LANES) if packed else (channels, 2 * band, wide // 2)
    taken = (step, LANES if packed else wide, raw_length)
    at = wide // LANES if packed else 0
    smem = pl.BlockSpec(memory_space=pltpu.SMEM)
    out_block = pl.BlockSpec((step,) + shape[1:], lambda i: (i, 0, 0))
    return pl.pallas_call(
        lambda *refs: spectra_kernel(packed, band, *refs),
        grid=(channels // step,),
        in_specs=[
            smem,
            smem,
            pl.BlockSpec(table.shape, lambda i: (0, 0)),
            pl.BlockSpec(taken, lambda i: (i, at, 0)),
        ],
        out_specs=[out_block] * 2,
        out_shape=[jax.ShapeDtypeStruct(shape, jnp.bfloat16)] * 2,
        scratch_shapes=[pltpu.VMEM((raw_length, 12 * band), jnp.bfloat16)],
        compiler_params=pltpu.CompilerParams(vmem_limit_bytes=STREAM_LIMIT),
        cost_estimate=cost(5 if packed else 8),
        name="spectra",
    )(core, fir_taps, table, raw_trace)


def round_up(value, unit):
    return -(-value // unit) * unit


def templates_kernel(
    real_at, imag_at, cos0, sin0, cos1, sin1, real_ref, imag_ref,
    eff1_ref, eff2_ref, norm_ref, cos_ref, sin_ref, stage,
):
    bins, channels, templates = real_ref.shape
    chips = real_at.shape[0]
    per_chip = channels // chips
    unit = math.gcd(per_chip, 8)
    split = eff1_ref.shape[2]

    @pl.when(pl.program_id(0) == 0)
    def _():
        cos_ref[...] = cos0[...]
        sin_ref[...] = sin0[...]
        norm_ref[...] = jnp.zeros_like(norm_ref)
        stage[...] = jnp.zeros_like(stage)

    for f in range(bins):
        power = jnp.zeros((per_chip, templates), jnp.float32)
        for j in range(chips):
            here = pl.ds(j * per_chip, per_chip)
            cosine, sine = cos_ref[here, :], sin_ref[here, :]
            cos_ref[here, :] = cosine * cos1[here, :] - sine * sin1[here, :]
            sin_ref[here, :] = sine * cos1[here, :] + cosine * sin1[here, :]
            real = real_ref[f, here, :].astype(jnp.float32)
            imag = imag_ref[f, here, :].astype(jnp.float32)
            eff_real = (real * cosine + imag * sine).astype(jnp.bfloat16).astype(jnp.float32)
            eff_imag = (imag * cosine - real * sine).astype(jnp.bfloat16).astype(jnp.float32)
            power += eff_real * eff_real + eff_imag * eff_imag
            stage[pl.ds(pl.multiple_of(real_at[j], unit), per_chip), :] = eff_real
            stage[pl.ds(pl.multiple_of(imag_at[j], unit), per_chip), :] = eff_imag
        norm_ref[...] += jnp.sum(power, axis=0, keepdims=True)
        eff1_ref[f] = stage[:split].astype(jnp.bfloat16).T
        eff2_ref[f] = stage[split:].astype(jnp.bfloat16).T


def templates_call(templ_real, templ_imag, channel_mask, moveout, samples, order, early):
    band, channels, templates = templ_real.shape
    chips = order.shape[0]
    per_chip = channels // chips
    half1, half2 = (round_up(n * per_chip, LANES) for n in (early, chips - early))
    depths = [2 * half1, 2 * half2]
    is_early = order < early
    real_at = jnp.where(is_early, order * per_chip, 2 * half1 + (order - early) * per_chip)
    imag_at = real_at + jnp.where(is_early, half1, half2)
    unit = 2.0 * math.pi / samples
    weight = channel_mask.astype(jnp.float32)
    start = (FIRST_BIN * moveout % samples).astype(jnp.float32) * unit
    turn = (moveout % samples).astype(jnp.float32) * unit
    tables = (weight * jnp.cos(start), weight * jnp.sin(start), jnp.cos(turn), jnp.sin(turn))
    step = math.gcd(band, 8)
    full = pl.BlockSpec((channels, templates), lambda i: (0, 0))
    block = pl.BlockSpec((step, channels, templates), lambda i: (i, 0, 0))
    return pl.pallas_call(
        templates_kernel,
        grid=(band // step,),
        in_specs=[pl.BlockSpec(memory_space=pltpu.SMEM)] * 2 + [full] * 4 + [block] * 2,
        out_specs=[pl.BlockSpec((step, templates, d), lambda i: (i, 0, 0)) for d in depths]
        + [pl.BlockSpec((1, templates), lambda i: (0, 0))],
        out_shape=[jax.ShapeDtypeStruct((band, templates, d), jnp.bfloat16) for d in depths]
        + [jax.ShapeDtypeStruct((1, templates), jnp.float32)],
        scratch_shapes=[pltpu.VMEM((channels, templates), jnp.float32)] * 2
        + [pltpu.VMEM((sum(depths), templates), jnp.float32)],
        compiler_params=pltpu.CompilerParams(vmem_limit_bytes=STREAM_LIMIT),
        cost_estimate=cost(12),
        name="templates",
    )(real_at, imag_at, *tables, templ_real, templ_imag)


def inverse_table(samples, band):
    table = jnp.asarray(forward_table(samples, band).T, jnp.float32)
    high = table.astype(jnp.bfloat16)
    low = (table - high.astype(jnp.float32)).astype(jnp.bfloat16)
    return jnp.concatenate([high, high, low], axis=1)


def block_copies(blocks, staged, sems):
    copies = []
    first = 0
    for i, block in enumerate(blocks):
        count = block.shape[0]
        copies.append(pltpu.make_async_copy(block, staged.at[pl.ds(first, count)], sems.at[i]))
        first += count
    return copies


def unpack_blocks(blocks, copies, staged, spec, pitch):
    rows, lanes = staged.shape[1:]
    padded = spec.shape[0] // pitch - 1
    filled = staged.shape[0]

    def clear(c, carry):
        spec[pl.ds(pl.multiple_of(c * pitch, 8), rows), :] = jnp.zeros((rows, lanes), jnp.float32)
        return carry

    lax.fori_loop(filled, padded, clear, 0)
    energy = jnp.zeros((rows, lanes), jnp.float32)
    first = 0
    for block, copy in zip(blocks, copies):
        count = block.shape[0]
        copy.wait()

        def unpack(c, energy):
            value = staged[c].astype(jnp.float32)
            spec[pl.ds(pl.multiple_of(c * pitch, 8), rows), :] = value
            return energy + value * value

        energy = lax.fori_loop(first, first + count, unpack, energy, unroll=math.gcd(count, 10))
        first += count
    return jnp.sum(energy, axis=0, keepdims=True)


def cross_of(packed, eff_a, eff_b, spec, pitch, f, bin_at, band):
    padded = spec.shape[0] // pitch - 1
    lane = lax.broadcasted_iota(jnp.int32, (1, LANES), 1)
    if packed:
        left = spec[pl.ds(bin_at, padded, stride=pitch), :]
        right = jnp.where(lane < HALF, 1.0, -1.0) * pltpu.roll(left, HALF, 1)
        values = jnp.concatenate([left, right], axis=0).astype(jnp.bfloat16)
    else:
        real = spec[pl.ds(bin_at, padded, stride=pitch), :].astype(jnp.bfloat16)
        imag = spec[pl.ds(band + bin_at, padded, stride=pitch), :].astype(jnp.bfloat16)
        top = jnp.concatenate([real, imag], axis=1)
        bottom = jnp.concatenate([imag, -real], axis=1)
        values = jnp.concatenate([top, bottom], axis=0)
    eff = jnp.concatenate([eff_a[f], eff_b[f]], axis=0)
    return jnp.dot(eff, values, preferred_element_type=jnp.float32)


def early_kernel(packed, band, count, *refs):
    blocks = refs[:count]
    eff_a, eff_b, cross_ref, energy_ref, spec, staged, sems = refs[count:]
    rows = blocks[0].shape[1]
    pitch = rows + SKEW
    step = pl.program_id(0)

    @pl.when(step == 0)
    def _():
        copies = block_copies(blocks, staged, sems)
        for copy in copies:
            copy.start()
        energy_ref[...] = unpack_blocks(blocks, copies, staged, spec, pitch)

    bins = eff_a.shape[0]
    for f in range(bins):
        cross_ref[f] = cross_of(packed, eff_a, eff_b, spec, pitch, f, step * bins + f, band)


def late_kernel(packed, band, count, scale, *refs):
    blocks = refs[:count]
    (
        eff_a, eff_b, partial_hbm, energy_in, norm_ref, table_ref, peak_ref, best_ref,
        spec, cross, energy_ref, staged, sems, partial_ref, partial_sems,
    ) = refs[count:]
    rows = blocks[0].shape[1]
    pitch = rows + SKEW
    lanes = LANES
    step = pl.program_id(0)
    bins, templates, _ = eff_a.shape
    group = templates if packed else 2 * templates
    depth = 2 * band
    cross_pitch = depth + SKEW
    lane = lax.broadcasted_iota(jnp.int32, (1, lanes), 1)

    def partial_copy(i):
        here = pl.ds(i * bins, bins)
        return pltpu.make_async_copy(partial_hbm.at[here], partial_ref.at[here], partial_sems.at[i])

    @pl.when(step == 0)
    def _():
        copies = block_copies(blocks, staged, sems)
        for copy in copies:
            copy.start()
        for i in range(partial_ref.shape[0] // bins):
            partial_copy(i).start()
        energy_ref[...] = energy_in[...] + unpack_blocks(blocks, copies, staged, spec, pitch)

    partial_copy(step).wait()

    for f in range(bins):
        at = step * bins + f
        out = partial_ref[at] + cross_of(packed, eff_a, eff_b, spec, pitch, f, at, band)
        if packed:
            first, second = out[:group], out[group:]
            real = jnp.where(lane < HALF, first, pltpu.roll(second, HALF, 1))
            imag = jnp.where(lane < HALF, pltpu.roll(first, HALF, 1), second)
        else:
            real, imag = out[:, :lanes], out[:, lanes:]
        cross[pl.ds(at, group, stride=cross_pitch), :] = real
        cross[pl.ds(band + at, group, stride=cross_pitch), :] = imag

    @pl.when(step == pl.num_programs(0) - 1)
    def _():
        def one_pair(i, carry):
            pair = jnp.concatenate(
                [
                    cross[pl.ds(pl.multiple_of((2 * i + j) * cross_pitch, 8), depth), :]
                    for j in range(2)
                ],
                axis=1,
            )
            high = pair.astype(jnp.bfloat16)
            low = (pair - high.astype(jnp.float32)).astype(jnp.bfloat16)
            values = jnp.concatenate([high, low, high], axis=0)
            out = jnp.dot(table_ref[...], values, preferred_element_type=jnp.float32)
            top = jnp.max(out, axis=0, keepdims=True)
            peak_ref[pl.ds(2 * i, 1), :] = top[:, :lanes]
            peak_ref[pl.ds(2 * i + 1, 1), :] = top[:, lanes:]
            return carry

        lax.fori_loop(0, group // 2, one_pair, 0, unroll=math.gcd(group // 2, 32))
        energy = energy_ref[...]
        norm = norm_ref[...]
        if packed:
            energy = energy + pltpu.roll(energy, HALF, 1)
            templ_norm = jnp.where(lane < HALF, norm[:group], norm[group:])
        else:
            templ_norm = norm
        data_norm = jnp.sqrt(energy + epsilon)
        peak = peak_ref[...] * scale / (templ_norm * data_norm)
        peak_ref[...] = peak
        best = jnp.max(peak, axis=0, keepdims=True)
        if packed:
            best = jnp.maximum(best, pltpu.roll(best, HALF, 1))
        best_ref[...] = best


def whole_block(array):
    return pl.BlockSpec(array.shape, lambda i: (0,) * array.ndim, pipeline_mode=pl.Buffered(1))


def early_call(packed, blocks, eff_a, eff_b):
    band, templates, depth = eff_a.shape
    rows = blocks[0].shape[1]
    step = math.gcd(band, 8)
    wide = LANES if packed else 2 * LANES
    eff_spec = pl.BlockSpec((step, templates, depth), lambda i: (i, 0, 0))
    hbm = pl.BlockSpec(memory_space=pltpu.HBM)
    return pl.pallas_call(
        lambda *refs: early_kernel(packed, band, len(blocks), *refs),
        grid=(band // step,),
        in_specs=[hbm] * len(blocks) + [eff_spec] * 2,
        out_specs=[
            pl.BlockSpec((step, 2 * templates, wide), lambda i: (i, 0, 0)),
            pl.BlockSpec((1, LANES), lambda i: (0, 0)),
        ],
        out_shape=[
            jax.ShapeDtypeStruct((band, 2 * templates, wide), jnp.float32),
            jax.ShapeDtypeStruct((1, LANES), jnp.float32),
        ],
        scratch_shapes=[
            pltpu.VMEM(((depth // 2 + 1) * (rows + SKEW), LANES), jnp.float32),
            pltpu.VMEM((sum(b.shape[0] for b in blocks), rows, LANES), jnp.bfloat16),
            pltpu.SemaphoreType.DMA((len(blocks),)),
        ],
        compiler_params=pltpu.CompilerParams(vmem_limit_bytes=PACKED_LIMIT if packed else WIDE_LIMIT),
        cost_estimate=cost(10),
        name="early",
    )(*blocks, eff_a, eff_b)


def late_call(packed, blocks, eff_a, eff_b, partial, energy, norm, table, scale):
    band, templates, depth = eff_a.shape
    rows = blocks[0].shape[1]
    step = math.gcd(band, 8)
    group = templates if packed else 2 * templates
    eff_spec = pl.BlockSpec((step, templates, depth), lambda i: (i, 0, 0))
    hbm = pl.BlockSpec(memory_space=pltpu.HBM)
    return pl.pallas_call(
        lambda *refs: late_kernel(packed, band, len(blocks), scale, *refs),
        grid=(band // step,),
        in_specs=[hbm] * len(blocks)
        + [eff_spec] * 2
        + [hbm]
        + [whole_block(a) for a in (energy, norm, table)],
        out_specs=[
            pl.BlockSpec((group, LANES), lambda i: (0, 0)),
            pl.BlockSpec((1, LANES), lambda i: (0, 0)),
        ],
        out_shape=[
            jax.ShapeDtypeStruct((group, LANES), jnp.float32),
            jax.ShapeDtypeStruct((1, LANES), jnp.float32),
        ],
        scratch_shapes=[
            pltpu.VMEM(((depth // 2 + 1) * (rows + SKEW), LANES), jnp.float32),
            pltpu.VMEM(((group + 1) * (2 * band + SKEW), LANES), jnp.float32),
            pltpu.VMEM((1, LANES), jnp.float32),
            pltpu.VMEM((sum(b.shape[0] for b in blocks), rows, LANES), jnp.bfloat16),
            pltpu.SemaphoreType.DMA((len(blocks),)),
            pltpu.VMEM(partial.shape, jnp.float32),
            pltpu.SemaphoreType.DMA((band // step,)),
        ],
        compiler_params=pltpu.CompilerParams(vmem_limit_bytes=PACKED_LIMIT if packed else LATE_LIMIT),
        cost_estimate=cost(14),
        name="late",
    )(*blocks, eff_a, eff_b, partial, energy, norm, table)


class Grid:
    def __init__(self, size):
        self.size = size
        self.core = 2
        outer = size // self.core
        self.y = 2 if outer % 2 == 0 else 1
        self.z = outer // self.y

    def place(self, z, y, c):
        return (z * self.y + y) * self.core + c

    @property
    def chips(self):
        return self.z * self.y

    def ring(self):
        turn = [z * self.y for z in range(self.z)]
        if self.y == 2:
            turn += [z * 2 + 1 for z in reversed(range(self.z))]
        return turn

    def ring_pairs(self, sign):
        turn = self.ring()
        return [
            (turn[i] * self.core + c, turn[(i + sign) % len(turn)] * self.core + c)
            for i in range(len(turn))
            for c in range(self.core)
        ]

    def swap_pairs(self):
        return [(i, i ^ 1) for i in range(self.size)]

    def z_pairs(self, distance):
        return [
            (self.place(z, y, c), self.place(z ^ distance, y, c))
            for z in range(self.z)
            for y in range(self.y)
            for c in range(self.core)
        ]

    def square_pairs(self):
        return [
            (self.place(z, y, c), self.place(z ^ 1, 1 - y, c))
            for z in range(self.z)
            for y in range(self.y)
            for c in range(self.core)
        ]

    def y_pairs(self):
        return [
            (self.place(z, y, c), self.place(z, 1 - y, c))
            for z in range(self.z)
            for y in range(self.y)
            for c in range(self.core)
        ]


def body(raw_trace, fir_taps, templ_real, templ_imag, channel_mask, moveout, *, row):
    grid = Grid(row)
    chips = grid.chips
    local_channels, windows, raw_length = raw_trace.shape
    samples = raw_length // 2
    band, channels, local_templates = templ_real.shape
    wide = windows // 2 // LANES * LANES
    index = lax.axis_index("row")
    core = index % grid.core
    first = core == 0

    def swap(value):
        return lax.ppermute(value, "row", grid.swap_pairs())

    def chip_block(keep, got):
        return jnp.stack([jnp.where(first, keep, got), jnp.where(first, got, keep)])

    core_table = core[None].astype(jnp.int32)
    p_keep, p_send = spectra_call(False, raw_trace, fir_taps, core_table, band)
    p_own = chip_block(p_keep, swap(p_send))
    turn = np.asarray(grid.ring())
    arrival = [0]
    for s in range(1, (chips - 1) // 2 + 1):
        arrival += [-s, s]
    if chips % 2 == 0:
        arrival.append(chips // 2)
    last_step = chips // 2
    early_steps = chips // 4
    early = 1 + 2 * early_steps
    rank = np.zeros((chips, chips), np.int32)
    for i in range(chips):
        for k, away in enumerate(arrival):
            rank[turn[i], turn[(i + away) % chips]] = k
    order = jnp.asarray(rank)[index // grid.core]

    raw_trace, templ_real, templ_imag, channel_mask, moveout, p_own = lax.optimization_barrier(
        (raw_trace, templ_real, templ_imag, channel_mask, moveout, p_own)
    )
    q_keep, q_send = spectra_call(True, raw_trace, fir_taps, core_table, band)
    eff1, eff2, norm = templates_call(
        templ_real, templ_imag, channel_mask, moveout, samples, order, early
    )
    table = inverse_table(samples, band)
    scale = math.sqrt(2.0 * channels * band)

    def forth(value):
        return lax.ppermute(value, "row", grid.ring_pairs(1))

    def back(value):
        return lax.ppermute(value, "row", grid.ring_pairs(-1))

    def flat(block):
        return block.reshape((-1,) + block.shape[-2:])

    def step(up, down, s):
        if 2 * s == chips:
            return forth(up[0]), back(down[1])
        return forth(up), back(down)

    def early_part(packed, blocks):
        return early_call(packed, [flat(b) for b in blocks], eff1, eff1_other)

    def late_part(packed, blocks, partial, energy):
        return late_call(
            packed, [flat(b) for b in blocks], eff2, eff2_other, partial, energy, templ_norm, table, scale
        )

    tie = lax.optimization_barrier
    p_blocks, q_blocks = [p_own], []
    p_up = p_down = p_own
    for s in range(1, last_step + 1):
        if s == last_step:
            p_early = early_part(False, p_blocks[:early])
            p_up, p_down, q_up, q_down, p_early = tie((p_up, p_down, q_up, q_down, p_early))
        p_up, p_down = step(p_up, p_down, s)
        p_blocks += [p_up, p_down]
        if s == 1:
            q_keep, q_send, p_up, p_down = tie((q_keep, q_send, p_up, p_down))
            q_own = chip_block(q_keep, swap(q_send))
            q_blocks.append(q_own)
            q_up = q_down = q_own
        elif s < last_step:
            q_up, q_down = step(q_up, q_down, s - 1)
            q_blocks += [q_up, q_down]
        if s == 2:
            eff1, eff2, norm, p_up, p_down, q_up, q_down = tie(
                (eff1, eff2, norm, p_up, p_down, q_up, q_down)
            )
            eff1_other, eff2_other = swap(eff1), swap(eff2)
            norm_pair = jnp.stack([norm[0], swap(norm)[0]])
            templ_norm = jnp.sqrt(norm_pair + epsilon).reshape(2 * local_templates, 1)
    q_up, q_down = step(q_up, q_down, last_step - 1)
    q_early = early_part(True, q_blocks[:early])
    p_up, p_down, q_up, q_down, q_early = tie((p_up, p_down, q_up, q_down, q_early))
    p_blocks[-2:] = [p_up, p_down]
    q_blocks += [q_up, q_down]
    q_blocks += step(q_up, q_down, last_step)
    p_peak, p_best = late_part(False, p_blocks[early:], *p_early)
    q_peak, q_best = late_part(True, q_blocks[early:], *q_early)

    p_other = swap(p_peak[local_templates:])
    q_other = swap(q_peak[:, HALF:])
    q_mine = q_peak[:, :HALF]
    p_mine = p_peak[:local_templates]
    peak = jnp.concatenate(
        [
            jnp.where(first, p_mine, p_other),
            jnp.where(first, p_other, p_mine),
            jnp.where(first, q_mine, q_other),
            jnp.where(first, q_other, q_mine),
        ],
        axis=1,
    )

    mine = jnp.concatenate([p_best, q_best], axis=1)
    distance = 1
    if grid.y == 2 and grid.z % 2 == 0:
        others = [grid.y_pairs(), grid.z_pairs(1), grid.square_pairs()]
        for got in [lax.ppermute(mine, "row", pairs) for pairs in others]:
            mine = jnp.maximum(mine, got)
        distance = 2
    elif grid.y == 2:
        mine = jnp.maximum(mine, lax.ppermute(mine, "row", grid.y_pairs()))
    if grid.z & (grid.z - 1) == 0:
        while distance < grid.z:
            mine = jnp.maximum(mine, lax.ppermute(mine, "row", grid.z_pairs(distance)))
            distance *= 2
    else:
        mine = lax.pmax(mine, "row")
    mine, peak = tie((mine, peak))
    other = swap(mine)
    one = jnp.where(first, mine, other)[0]
    two = jnp.where(first, other, mine)[0]
    best = jnp.concatenate(
        [one[:wide], two[:wide], one[wide : wide + HALF], two[wide : wide + HALF]]
    )
    return (peak, best)


def solution(mesh):
    in_specs = (
        P("row", "parts", None),
        P(),
        P(None, None, "row"),
        P(None, None, "row"),
        P(None, "row"),
        P(None, "row"),
    )
    out_specs = (P("row", "parts"), P("parts"))
    row = mesh.shape["row"]

    def local(*args):
        return body(*args, row=row)

    return jax.shard_map(local, mesh=mesh, in_specs=in_specs, out_specs=out_specs, check_vma=False)
```
